128 devices in a mesh: grp: 8 (over z, core), sub: 16 (over x, y).
Axes of the slice: x: 4, y: 4, z: 4, core: 2. Of those that a mesh axis runs over, the one named last changes fastest.
Arguments:
- basis: bfloat16 [3, 262144, 512], P(None, ('grp', 'sub')), may hold values from -0.25 to 0.25
- observations: bfloat16 [262144], P(('grp', 'sub')), may hold values from -6 to 6
- counts: int32 [128], P(('grp', 'sub')), may hold values from 1024 to 2048, as said below
- noise_prec: float32 [128], P(('grp', 'sub')), may hold values from 0.5 to 4
- prior_fine: float32 [128, 512, 512], P(('grp', 'sub')), as said below
- prior_group: float32 [8, 512, 512], P('grp'), as said below
- prior_root: float32 [512, 512], replicated, as said below
Outputs:
- mean_root: float32 [512], P('sub')
- mean_group: float32 [4096], P(('grp', 'sub'))
- mean_fine: float32 [65536], P(('grp', 'sub'))
- fitted: float32 [262144], P(('grp', 'sub'))
The draws below stay inside these ranges and needn't reach their ends.
Inputs may be any that keep to these rules, and one draw needn't show every extreme that they name: `counts`: valid observations of each finest region; some region has exactly 2048, some exactly 1024. `prior_fine`: each block is a symmetric positive definite precision matrix. `prior_group`: each block is a symmetric positive definite precision matrix. `prior_root`: a symmetric positive definite precision matrix.
All inputs are finite; a program needn't handle non-finite values.
Results may differ from the reference program's by a relative error of at most 0.003.
Values sent between devices are 32-bit elements; how exact they have to be, the bound alone decides.
A program may use at most 128 MiB of HBM per device.

```python
import math
import jax
import jax.numpy as jnp
from jax import lax

R = 512
NOBS = 2048
LEVELS = 3
GROUPS = 8
REGIONS = 128


def precision_blocks(key, lead, width, top):
    first, second = jax.random.split(key)
    diagonal = jnp.exp(jax.random.uniform(first, (lead, width), jnp.float32, 0.0, math.log(top)))
    bound = 0.9 / width
    offdiag = jax.random.uniform(second, (lead, width, width), jnp.float32, -bound, bound)
    offdiag = 0.5 * (offdiag + jnp.swapaxes(offdiag, 1, 2))
    square = jnp.arange(width)[:, None] == jnp.arange(width)[None, :]
    return jnp.where(square[None], diagonal[:, :, None], offdiag)


def draw_prior_fine(key, part):
    key = jax.random.fold_in(key, 11)
    top = 8.0
    return precision_blocks(key, REGIONS, R, top)


def draw_prior_group(key, part):
    key = jax.random.fold_in(key, 12)
    top = 8.0
    return precision_blocks(key, GROUPS, R, top)


def draw_prior_root(key, part):
    key = jax.random.fold_in(key, 13)
    top = 8.0
    return precision_blocks(key, 1, R, top)[0]


def draw_counts(key, part):
    key = jax.random.fold_in(key, 14)
    first, second, third = jax.random.split(key, 3)
    values = jax.random.randint(first, (REGIONS,), NOBS // 2, NOBS + 1)
    where_top = jax.random.randint(second, (), 0, REGIONS)
    where_low = (where_top + 1 + jax.random.randint(third, (), 0, REGIONS - 1)) % REGIONS
    values = values.at[where_top].set(NOBS)
    values = values.at[where_low].set(NOBS // 2)
    return values.astype(jnp.int32)


def levels(own_key, shape, shards, low, high):
    def one(position, blocks):
        steps = jax.random.uniform(jax.random.fold_in(jax.random.fold_in(own_key, 6), position), (blocks,), jnp.float32, low / len(shards), high / len(shards))
        return jnp.repeat(jnp.exp(steps), shape[position] // blocks).reshape((-1,) + (1,) * (len(shape) - position - 1))

    factor_of = one(*shards[0])
    for cut in shards[1:]:
        factor_of = factor_of * one(*cut)
    return factor_of


def noise(key, shape, spread, reach, cuts=(), kind=jnp.bfloat16):
    values = jax.random.normal(key, shape, jnp.float32) * spread
    if len(cuts) > 0:
        values = levels(key, shape, cuts, -0.22, 0.18) * values
    return jnp.clip(values, min=-reach, max=reach).astype(kind)


def setup_inputs(seed: int = 0) -> dict:
    seeds = jax.random.split(jax.random.key(seed), 8)
    return {
        "basis": noise(seeds[0], (LEVELS, REGIONS * NOBS, R), R ** -0.5, 0.25, ((1, 128),)),
        "observations": noise(seeds[1], (REGIONS * NOBS,), 1.0, 6.0, ((0, 128),)),
        "counts": draw_counts(jax.random.fold_in(seeds[7], 71), 0),
        "noise_prec": jnp.clip(jnp.exp(math.log(4.0) - 2.0794415 * jax.random.uniform(seeds[3], (REGIONS,), jnp.float32) ** levels(seeds[3], (REGIONS,), ((0, 128),), -0.2, 0.2)), 0.5, 4.0),
        "prior_fine": draw_prior_fine(jax.random.fold_in(seeds[7], 71), 0),
        "prior_group": draw_prior_group(jax.random.fold_in(seeds[7], 71), 0),
        "prior_root": draw_prior_root(jax.random.fold_in(seeds[7], 71), 0),
    }


def solve_lower(lower, rhs, trans=False):
    if rhs.ndim == 1:
        return lax.linalg.triangular_solve(lower, rhs[:, None], left_side=True, lower=True, transpose_a=trans)[:, 0]
    return lax.linalg.triangular_solve(lower, rhs, left_side=True, lower=True, transpose_a=trans)

def tdot(left, right):
    return lax.dot_general(left.astype(jnp.float32), right.astype(jnp.float32), (((0,), (0,)), ((), ())), precision=lax.Precision.HIGHEST, preferred_element_type=jnp.float32)

def bdot(left, right):
    return lax.dot_general(left.astype(jnp.float32), right.astype(jnp.float32), (((0,), (0,)), ((), ())), preferred_element_type=jnp.float32)

def fine_partials(args):
    bases, obs, count, tau, prior = args
    valid = (jnp.arange(NOBS, dtype=jnp.int32) < count).astype(jnp.bfloat16)
    masked = bases * valid[None, :, None]
    ymask = obs * valid
    g22 = tau * bdot(masked[2], bases[2])
    g21 = tau * bdot(masked[2], bases[1])
    g20 = tau * bdot(masked[2], bases[0])
    g11 = tau * bdot(masked[1], bases[1])
    g10 = tau * bdot(masked[1], bases[0])
    g00 = tau * bdot(masked[0], bases[0])
    v2 = tau * bdot(bases[2], ymask)
    v1 = tau * bdot(bases[1], ymask)
    v0 = tau * bdot(bases[0], ymask)
    lower2 = jnp.linalg.cholesky(prior + g22)
    upper0 = solve_lower(lower2, g20)
    upper1 = solve_lower(lower2, g21)
    small = solve_lower(lower2, v2)
    s11 = g11 - tdot(upper1, upper1)
    s10 = g10 - tdot(upper1, upper0)
    s00 = g00 - tdot(upper0, upper0)
    t1 = v1 - tdot(upper1, small)
    t0 = v0 - tdot(upper0, small)
    return (s11, s10, s00, t1, t0, lower2, upper0, upper1, small)

def group_level(args):
    prior, s11, s10, s00, t1, t0 = args
    lower1 = jnp.linalg.cholesky(prior + jnp.sum(s11, axis=0))
    coupled = solve_lower(lower1, jnp.sum(s10, axis=0))
    vector = solve_lower(lower1, jnp.sum(t1, axis=0))
    reduced = jnp.sum(s00, axis=0) - tdot(coupled, coupled)
    rvector = jnp.sum(t0, axis=0) - tdot(coupled, vector)
    return (reduced, rvector, lower1, coupled, vector)

def reference(basis, observations, counts, noise_prec, prior_fine, prior_group, prior_root):
    regions = counts.shape[0]
    groups = prior_group.shape[0]
    per = regions // groups
    bases = jnp.swapaxes(basis.reshape(LEVELS, regions, NOBS, R), 0, 1)
    obs = observations.reshape(regions, NOBS)
    s11, s10, s00, t1, t0, lower2, upper0, upper1, small = lax.map(fine_partials, (bases, obs, counts, noise_prec, prior_fine))

    def split(x):
        return x.reshape((groups, per) + x.shape[1:])
    reduced, rvector, lower1, coupled, vector = lax.map(group_level, (prior_group, split(s11), split(s10), split(s00), split(t1), split(t0)))
    lower0 = jnp.linalg.cholesky(prior_root + jnp.sum(reduced, axis=0))
    mean_root = solve_lower(lower0, solve_lower(lower0, jnp.sum(rvector, axis=0)), True)

    def group_mean(args):
        low, cpl, vec = args
        rhs = vec - jnp.dot(cpl, mean_root, precision=lax.Precision.HIGHEST)
        return solve_lower(low, rhs, True)
    mean_group = lax.map(group_mean, (lower1, coupled, vector))
    parent = jnp.repeat(mean_group, per, axis=0)

    def fine_mean(args):
        low, up0, up1, vec, pmean, bas = args
        rhs = vec - jnp.dot(up0, mean_root, precision=lax.Precision.HIGHEST) - jnp.dot(up1, pmean, precision=lax.Precision.HIGHEST)
        mean2 = solve_lower(low, rhs, True)
        field = jnp.dot(bas[0].astype(jnp.float32), mean_root.astype(jnp.bfloat16).astype(jnp.float32), preferred_element_type=jnp.float32)
        field = field + jnp.dot(bas[1].astype(jnp.float32), pmean.astype(jnp.bfloat16).astype(jnp.float32), preferred_element_type=jnp.float32)
        field = field + jnp.dot(bas[2].astype(jnp.float32), mean2.astype(jnp.bfloat16).astype(jnp.float32), preferred_element_type=jnp.float32)
        return (mean2, field)
    mean_fine, fitted = lax.map(fine_mean, (lower2, upper0, upper1, small, parent, bases))
    return (mean_root, mean_group.reshape(-1), mean_fine.reshape(-1), fitted.reshape(-1))
```

```python
import functools

import jax
import jax.numpy as jnp
from jax import lax
from jax.experimental import pallas as pl
from jax.experimental.pallas import tpu as pltpu
from jax.sharding import PartitionSpec as P

F32 = jnp.float32
BF = jnp.bfloat16
R = 512
NB = 16
VM = pl.BlockSpec(memory_space=pltpu.VMEM)
SM = pl.BlockSpec(memory_space=pltpu.SMEM)
NN = (((1,), (0,)), ((), ()))
TN = (((0,), (0,)), ((), ()))
NT = (((1,), (1,)), ((), ()))


def split2(x):
    high = x.astype(BF)
    return high, (x - high.astype(F32)).astype(BF)


def split3(x):
    high = x.astype(BF)
    rest = x - high.astype(F32)
    mid = rest.astype(BF)
    return high, mid, (rest - mid.astype(F32)).astype(BF)


def dot(left, right, dims):
    return lax.dot_general(left, right, dims, preferred_element_type=F32)


def dot3(left, right, dims):
    a, b = left if isinstance(left, tuple) else split2(left)
    c, d = right if isinstance(right, tuple) else split2(right)
    return dot(a, c, dims) + (dot(a, d, dims) + dot(b, c, dims))


def rank_update(rows, panel):
    a, b, c = split3(rows)
    d, e, f = split3(panel)
    return dot(jnp.concatenate([a, a, b, a, b, c], 0), jnp.concatenate([d, e, d, f, e, d], 0), TN)


def sweep_panel(mat, tile, q):
    n = mat.shape[1]
    row0 = pl.multiple_of(tile * 128 + q * NB, NB)
    lane0 = pl.multiple_of(tile * 128, 128)
    rows = mat[pl.ds(row0, NB), :]
    diag = mat[pl.ds(row0, NB), pl.ds(lane0, 128)]
    halves = NB // 8
    sub = lax.broadcasted_iota(jnp.int32, (8, 128), 0)
    lane = lax.broadcasted_iota(jnp.int32, (8, 128), 1)
    cols = [
        [jnp.broadcast_to(diag[8 * h : 8 * h + 8, q * NB + j : q * NB + j + 1], (8, 128)) for h in range(halves)]
        for j in range(NB)
    ]
    inside = (lane >= q * NB) & (lane < q * NB + NB)
    work = []
    for c in range(n // 128):
        part = []
        for h in range(halves):
            eye = jnp.where(lane == q * NB + 8 * h + sub, -1.0, 0.0)
            part.append(jnp.where(inside & (tile == c), eye, rows[8 * h : 8 * h + 8, c * 128 : c * 128 + 128]))
        work.append(part)
    for i in range(NB):
        hi, si = divmod(i, 8)
        inv = 1.0 / jnp.broadcast_to(cols[i][hi][si : si + 1, :], (8, 128))
        mult = [-cols[i][h] * inv for h in range(halves)]
        mult[hi] = jnp.where(sub == si, inv, mult[hi])

        def step(vec):
            pivot_row = jnp.broadcast_to(vec[hi][si : si + 1, :], (8, 128))
            out = []
            for h in range(halves):
                base = jnp.where(sub == si, 0.0, vec[h]) if h == hi else vec[h]
                out.append(base + mult[h] * pivot_row)
            return out

        for j in range(i + 1, NB):
            cols[j] = step(cols[j])
        work = [step(part) for part in work]
    panel = jnp.concatenate([jnp.concatenate([part[h] for part in work], 1) for h in range(halves)], 0)
    lane1 = lax.broadcasted_iota(jnp.int32, (1, 128), 1)
    mask = (lane1 >= q * NB) & (lane1 < q * NB + NB)
    mat[:, pl.ds(lane0, 128)] = jnp.where(mask, 0.0, mat[:, pl.ds(lane0, 128)])
    mat[...] = mat[...] - rank_update(rows, panel)
    mat[pl.ds(row0, NB), :] = panel


def negative_inverse(mat):
    def body(tile, carry):
        for q in range(128 // NB):
            sweep_panel(mat, tile, q)
        return carry

    lax.fori_loop(0, mat.shape[0] // 128, body, 0)


def row_dot(vec, mat):
    a, b, c = [part.astype(F32) for part in split3(vec)]
    index = lax.broadcasted_iota(jnp.int32, (16, vec.shape[1]), 0)
    left = jnp.where(index == 0, a, jnp.where(index == 1, b, jnp.where(index == 2, c, 0.0))).astype(BF)
    high, low = split2(mat)
    out = dot(left, high, NN) + dot(left, low, NN)
    return jnp.sum(out, axis=0, keepdims=True)


def fine_kernel(count, tau, basis, obs, prior, s11, s01, s00, svec, xneg, mat, cross):
    slots = basis.shape[1]
    t = tau[0]
    valid = lax.broadcasted_iota(jnp.int32, (slots, 1), 0) < count[0]
    yvalid = lax.broadcasted_iota(jnp.int32, (1, slots), 1) < count[0]
    y = jnp.where(yvalid, obs[...].astype(F32), 0.0)
    y = jnp.where(lax.broadcasted_iota(jnp.int32, (16, slots), 0) == 0, y, 0.0).astype(BF)

    def masked(a):
        block = basis[a]
        return jnp.where(valid, block, jnp.zeros_like(block))

    m2 = masked(2)
    mat[...] = prior[0] + t * dot(basis[2], m2, TN)
    cross[0:R, :] = t * dot(basis[1], m2, TN)
    cross[R : 2 * R, :] = t * dot(basis[0], m2, TN)
    cross[2 * R : 2 * R + 16, :] = t * dot(y, m2, NN)
    m1 = masked(1)
    s11[...] = t * dot(basis[1], m1, TN)
    s01[...] = t * dot(basis[0], m1, TN)
    svec[0:16, :] = t * dot(y, m1, NN)
    m0 = masked(0)
    s00[...] = t * dot(basis[0], m0, TN)
    svec[16:32, :] = t * dot(y, m0, NN)
    negative_inverse(mat)
    inv = split2(mat[...])
    c1 = split2(cross[0:R, :])
    c0 = split2(cross[R : 2 * R, :])
    x1 = dot3(c1, inv, NN)
    xneg[0:R, :] = x1
    s11[...] = s11[...] + dot3(x1, c1, NT)
    x0 = dot3(c0, inv, NN)
    xneg[R : 2 * R, :] = x0
    x0 = split2(x0)
    s01[...] = s01[...] + dot3(x0, c1, NT)
    s00[...] = s00[...] + dot3(x0, c0, NT)
    xy = dot3(cross[2 * R : 2 * R + 16, :], inv, NN)
    xneg[2 * R : 2 * R + 16, :] = xy
    svec[0:16, :] = svec[0:16, :] + dot3(xy, c1, NT)
    svec[16:32, :] = svec[16:32, :] + dot3(xy, c0, NT)


def group_kernel(prior, a11, a01, a1, s00, s0, inv1, part, pvec):
    place = lax.axis_index("sub")
    inv1[...] = prior[0] + a11[...]
    negative_inverse(inv1)
    lanes = R // lax.axis_size("sub")
    tile = pl.multiple_of(lax.div(place * lanes, 128) * 128, 128)
    first = place * lanes - tile
    lane = lax.broadcasted_iota(jnp.int32, (1, 128), 1)
    mask = (lane >= first) & (lane < first + lanes)
    cols = split2(jnp.where(mask, inv1[:, pl.ds(tile, 128)], 0.0))
    mine = split2(a01[:, pl.ds(tile, 128)])
    x = dot3(a01[...], cols, NN)
    part[...] = s00[...] + dot3(x, mine, NT)
    xv = dot3(a1[...], cols, NN)
    pvec[...] = s0[...] + dot3(xv, mine, NT)


def root_kernel(prior, a0, b0, inv1, a01, a1, xneg, basis, root, group, fine, field, mat):
    mat[...] = prior[...] + a0[...]
    negative_inverse(mat)
    mean0 = -row_dot(b0[0:1, :], mat[...])
    root[...] = mean0
    mean1 = -row_dot(a1[0:1, :] - row_dot(mean0, a01[...]), inv1[...])
    group[...] = mean1
    mean2 = row_dot(mean1, xneg[0:R, :]) + row_dot(mean0, xneg[R : 2 * R, :]) - xneg[2 * R : 2 * R + 1, :]
    fine[...] = mean2

    def fit(mean, a):
        left = jnp.broadcast_to(mean, (16, R)).astype(BF)
        return dot(left, basis[a], NT)

    field[...] = (fit(mean0, 0) + fit(mean1, 1) + fit(mean2, 2))[0:1, :]


def shape(*dims):
    return jax.ShapeDtypeStruct(dims, F32)


PARAMS = dict(vmem_limit_bytes=56 << 20)


def shards(basis, observations, counts, noise_prec, prior_fine, prior_group, prior_root):
    slots = basis.shape[1]
    s11, s01, s00, svec, xneg = pl.pallas_call(
        fine_kernel,
        name="fine",
        out_shape=[shape(R, R), shape(R, R), shape(R, R), shape(32, R), shape(2 * R + 16, R)],
        in_specs=[SM, SM, VM, VM, VM],
        out_specs=[VM] * 5,
        scratch_shapes=[pltpu.VMEM((R, R), F32), pltpu.VMEM((2 * R + 16, R), F32)],
        compiler_params=pltpu.CompilerParams(**PARAMS),
    )(counts, noise_prec, basis, observations.reshape(1, slots), prior_fine)
    a11, a01, a1 = lax.psum((s11, s01, svec[0:16]), "sub")
    inv1, part, pvec = pl.pallas_call(
        group_kernel,
        name="group",
        out_shape=[shape(R, R), shape(R, R), shape(16, R)],
        in_specs=[VM] * 6,
        out_specs=[VM] * 3,
        compiler_params=pltpu.CompilerParams(**PARAMS),
    )(prior_group, a11, a01, a1, s00, svec[16:32])
    a0, b0 = lax.psum((part, pvec), ("grp", "sub"))
    root, group, fine, field = pl.pallas_call(
        root_kernel,
        name="root",
        out_shape=[shape(1, R), shape(1, R), shape(1, R), shape(1, slots)],
        in_specs=[VM] * 8,
        out_specs=[VM] * 4,
        scratch_shapes=[pltpu.VMEM((R, R), F32)],
        compiler_params=pltpu.CompilerParams(**PARAMS),
    )(prior_root, a0, b0, inv1, a01, a1, xneg, basis)
    piece = R // lax.axis_size("sub")
    position = lax.axis_index("sub") * piece
    return (
        lax.dynamic_slice_in_dim(root[0], position, piece),
        lax.dynamic_slice_in_dim(group[0], position, piece),
        fine[0],
        field[0],
    )


def solution(mesh):
    in_specs = (
        P(None, ("grp", "sub"), None),
        P(("grp", "sub")),
        P(("grp", "sub")),
        P(("grp", "sub")),
        P(("grp", "sub"), None, None),
        P("grp", None, None),
        P(),
    )
    out_specs = (P("sub"), P(("grp", "sub")), P(("grp", "sub")), P(("grp", "sub")))
    return jax.shard_map(shards, mesh=mesh, in_specs=in_specs, out_specs=out_specs, check_vma=False)
```

```python
import functools

import jax
import jax.numpy as jnp
from jax import lax
from jax.experimental import pallas as pl
from jax.experimental.pallas import tpu as pltpu
from jax.sharding import PartitionSpec as P

F32 = jnp.float32
BF = jnp.bfloat16
MESH = pl.DeviceIdType.MESH
R = 512
NB = 16
VM = pl.BlockSpec(memory_space=pltpu.VMEM)
SM = pl.BlockSpec(memory_space=pltpu.SMEM)
NN = (((1,), (0,)), ((), ()))
TN = (((0,), (0,)), ((), ()))
NT = (((1,), (1,)), ((), ()))


def split2(x):
    high = x.astype(BF)
    return high, (x - high.astype(F32)).astype(BF)


def split3(x):
    high = x.astype(BF)
    rest = x - high.astype(F32)
    mid = rest.astype(BF)
    return high, mid, (rest - mid.astype(F32)).astype(BF)


def dot(left, right, dims):
    return lax.dot_general(left, right, dims, preferred_element_type=F32)


def dot3(left, right, dims):
    a, b = left if isinstance(left, tuple) else split2(left)
    c, d = right if isinstance(right, tuple) else split2(right)
    return dot(a, c, dims) + (dot(a, d, dims) + dot(b, c, dims))


def rank_update(rows, panel):
    a, b, c = split3(rows)
    d, e, f = split3(panel)
    return dot(jnp.concatenate([a, a, b, a, b, c], 0), jnp.concatenate([d, e, d, f, e, d], 0), TN)


def sweep_panel(mat, p):
    tiles = mat.shape[1] // 128
    row0 = pl.multiple_of(p * NB, NB)
    tile = lax.div(p * NB, 128)
    lane0 = pl.multiple_of(tile * 128, 128)
    first = p * NB - tile * 128
    rows = mat[pl.ds(row0, NB), :]
    diag = mat[pl.ds(row0, NB), pl.ds(lane0, 128)]
    sub = lax.broadcasted_iota(jnp.int32, (NB, 128), 0)
    lane = lax.broadcasted_iota(jnp.int32, (NB, 128), 1)
    cols = []
    for j in range(NB):
        col = jnp.sum(jnp.where(lane == first + j, diag, 0.0), axis=1, keepdims=True)
        cols.append(jnp.broadcast_to(col, (NB, 128)))
    inside = (lane >= first) & (lane < first + NB)
    eye = jnp.where(lane == first + sub, -1.0, 0.0)
    blocks = [jnp.where(inside & (tile == c), eye, rows[:, c * 128 : c * 128 + 128]) for c in range(tiles)]
    work = jnp.stack(cols + blocks, 0)
    for i in range(NB):
        inv = 1.0 / jnp.broadcast_to(work[0, i : i + 1, :], (NB, 128))
        mult = jnp.where(sub == i, inv, -work[0] * inv)
        work = work[1:]
        pivot_row = jnp.broadcast_to(work[:, i : i + 1, :], work.shape)
        work = jnp.where((sub == i)[None], 0.0, work) + mult[None] * pivot_row
    panel = jnp.concatenate([work[c] for c in range(tiles)], 1)
    lane1 = lax.broadcasted_iota(jnp.int32, (1, 128), 1)
    mask = (lane1 >= first) & (lane1 < first + NB)
    mat[:, pl.ds(lane0, 128)] = jnp.where(mask, 0.0, mat[:, pl.ds(lane0, 128)])
    mat[...] = mat[...] - rank_update(rows, panel)
    mat[pl.ds(row0, NB), :] = panel


def sweep_panels(mat, low, high):
    def body(p, carry):
        sweep_panel(mat, p)
        return carry

    lax.fori_loop(low, high, body, 0)


def negative_inverse(mat):
    sweep_panels(mat, 0, mat.shape[0] // NB)


def row_dot(vec, mat):
    a, b, c = [part.astype(F32) for part in split3(vec)]
    index = lax.broadcasted_iota(jnp.int32, (16, vec.shape[1]), 0)
    left = jnp.where(index == 0, a, jnp.where(index == 1, b, jnp.where(index == 2, c, 0.0))).astype(BF)
    high, low = split2(mat)
    out = dot(left, high, NN) + dot(left, low, NN)
    return jnp.sum(out, axis=0, keepdims=True)


def fine_kernel(count, tau, basis, obs, prior, s11, g01, g00, svec, cross, xneg, mat):
    slots = basis.shape[1]
    t = tau[0]
    valid = lax.broadcasted_iota(jnp.int32, (slots, 1), 0) < count[0]
    yvalid = lax.broadcasted_iota(jnp.int32, (1, slots), 1) < count[0]
    y = jnp.where(yvalid, obs[...].astype(F32), 0.0)
    y = jnp.where(lax.broadcasted_iota(jnp.int32, (16, slots), 0) == 0, y, 0.0).astype(BF)

    def masked(a):
        block = basis[a]
        return jnp.where(valid, block, jnp.zeros_like(block))

    m2 = masked(2)
    mat[...] = prior[0] + t * dot(basis[2], m2, TN)
    cross[0:R, :] = t * dot(basis[1], m2, TN)
    cross[R : 2 * R, :] = t * dot(basis[0], m2, TN)
    cross[2 * R : 2 * R + 16, :] = t * dot(y, m2, NN)
    m1 = masked(1)
    s11[...] = t * dot(basis[1], m1, TN)
    g01[...] = t * dot(basis[0], m1, TN)
    svec[0:16, :] = t * dot(y, m1, NN)
    m0 = masked(0)
    g00[...] = t * dot(basis[0], m0, TN)
    svec[16:32, :] = t * dot(y, m0, NN)
    negative_inverse(mat)
    inv = split2(mat[...])
    c1 = split2(cross[0:R, :])
    c0 = split2(cross[R : 2 * R, :])
    x1 = dot3(c1, inv, NN)
    xneg[0:R, :] = x1
    s11[...] = s11[...] + dot3(x1, c1, NT)
    xneg[R : 2 * R, :] = dot3(c0, inv, NN)
    xy = dot3(cross[2 * R : 2 * R + 16, :], inv, NN)
    xneg[2 * R : 2 * R + 16, :] = xy
    svec[0:16, :] = svec[0:16, :] + dot3(xy, c1, NT)
    svec[16:32, :] = svec[16:32, :] + dot3(xy, c0, NT)


SYM = 80
PIECE = SYM + 8


def segments():
    out = []
    flat = 0
    for i in range(R // 128):
        for j in range(i + 1):
            row = 0
            while row < 128:
                size = min(128 - row, SYM - flat % SYM)
                out.append((i, j, row, flat // SYM, flat % SYM, size))
                row += size
                flat += size
    return out


def pack(full, vec, pieces):
    pieces[:, SYM:PIECE, :] = jnp.zeros((pieces.shape[0], 8, 128), F32)
    for i, j, row, piece, at, size in segments():
        pieces[piece, at : at + size, :] = full[128 * i + row : 128 * i + row + size, 128 * j : 128 * j + 128]
    for c in range(R // 128):
        pieces[4 * c, SYM:PIECE, :] = vec[0:8, 128 * c : 128 * c + 128]


def unpack(pieces, full, vec):
    for i, j, row, piece, at, size in segments():
        full[128 * i + row : 128 * i + row + size, 128 * j : 128 * j + 128] = pieces[piece, at : at + size, :]
    for i in range(R // 128):
        for j in range(i):
            full[128 * j : 128 * j + 128, 128 * i : 128 * i + 128] = full[
                128 * i : 128 * i + 128, 128 * j : 128 * j + 128
            ].T
    for c in range(R // 128):
        vec[0:8, 128 * c : 128 * c + 128] = pieces[4 * c, SYM:PIECE, :]


class Exchange:
    def __init__(self, axis, source, into, send_sem, recv_sem):
        self.axis, self.source, self.into, self.send_sem, self.recv_sem = axis, source, into, send_sem, recv_sem
        self.n = lax.axis_size(axis)
        self.me = lax.axis_index(axis)

    def copy(self, d):
        peer = lax.rem(self.me + d, self.n)
        return pltpu.make_async_remote_copy(
            src_ref=self.source(peer),
            dst_ref=self.into(d),
            send_sem=self.send_sem.at[d],
            recv_sem=self.recv_sem.at[d],
            device_id={self.axis: peer},
            device_id_type=MESH,
        )

    def each(self, act):
        def body(d, carry):
            act(self.copy(d))
            return carry

        lax.fori_loop(1, self.n, body, 0)

    def start(self):
        self.each(lambda copy: copy.start())

    def wait_recv(self):
        self.each(lambda copy: copy.wait_recv())

    def wait_send(self):
        self.each(lambda copy: copy.wait_send())


def group_kernel(
    prior, s11, g01, g00, svec, cross, xneg,
    inv1_out, a01_out, a1_out, a0_out, b0_out,
    send1, recv1, all1, s01, recv01, a01, part, pvec, send0, recv0, mid0, recvg, all0,
    sem_s, sem_r, semg_s, semg_r,
):
    sub = lax.axis_index("sub")
    grp = lax.axis_index("grp")
    nsub, ngrp = lax.axis_size("sub"), lax.axis_size("grp")
    rows = R // nsub
    barrier = pltpu.get_barrier_semaphore()

    def greet(axis, me, n):
        def body(d, carry):
            pl.semaphore_signal(
                barrier, inc=1, device_id={axis: lax.rem(me + d, n)}, device_id_type=MESH
            )
            return carry

        lax.fori_loop(1, n, body, 0)

    greet("sub", sub, nsub)
    greet("grp", grp, ngrp)
    pack(s11, svec, send1)
    pl.semaphore_wait(barrier, nsub + ngrp - 2)

    slab = pl.ds(pl.multiple_of(sub * rows, rows), rows)
    scatter1 = Exchange("sub", lambda peer: send1.at[peer], lambda d: recv1.at[d], sem_s.at[0], sem_r.at[0])
    gather1 = Exchange("sub", lambda peer: all1.at[sub], lambda d: all1.at[sub], sem_s.at[1], sem_r.at[1])
    scatter01 = Exchange(
        "sub", lambda peer: s01.at[pl.ds(pl.multiple_of(peer * rows, rows), rows), :], lambda d: recv01.at[d],
        sem_s.at[2], sem_r.at[2],
    )
    gather01 = Exchange("sub", lambda peer: a01.at[slab, :], lambda d: a01.at[slab, :], sem_s.at[3], sem_r.at[3])
    scatter0 = Exchange("sub", lambda peer: send0.at[peer], lambda d: recv0.at[d], sem_s.at[4], sem_r.at[4])
    gather0 = Exchange("sub", lambda peer: all0.at[sub], lambda d: all0.at[sub], sem_s.at[5], sem_r.at[5])
    across = Exchange("grp", lambda peer: mid0, lambda d: recvg.at[d], semg_s, semg_r)

    scatter1.start()
    c1 = split2(cross[0:R, :])
    c0 = split2(cross[R : 2 * R, :])
    x0 = split2(xneg[R : 2 * R, :])
    s01[...] = g01[...] + dot3(x0, c1, NT)
    part[...] = g00[...] + dot3(x0, c0, NT)
    scatter1.wait_recv()
    all1[sub] = send1[sub] + jnp.sum(recv1[1:], axis=0)
    gather1.start()
    scatter01.start()
    gather1.wait_recv()
    unpack(all1, inv1_out, a1_out)
    inv1_out[...] = inv1_out[...] + prior[0]
    panels = R // NB
    cut = panels * 5 // 8
    sweep_panels(inv1_out, 0, cut)
    scatter01.wait_recv()
    a01[slab, :] = s01[slab, :] + jnp.sum(recv01[1:], axis=0)
    gather01.start()
    sweep_panels(inv1_out, cut, panels)
    gather01.wait_recv()

    tile = pl.multiple_of(lax.div(sub * rows, 128) * 128, 128)
    first = sub * rows - tile
    lane = lax.broadcasted_iota(jnp.int32, (1, 128), 1)
    mask = (lane >= first) & (lane < first + rows)
    cols = split2(jnp.where(mask, inv1_out[:, pl.ds(tile, 128)], 0.0))
    mine = split2(a01[:, pl.ds(tile, 128)])
    x = dot3(a01[...], cols, NN)
    part[...] = part[...] + dot3(x, mine, NT)
    xv = dot3(jnp.concatenate([a1_out[...], a1_out[...]], 0), cols, NN)
    pvec[...] = svec[16:32, :] + dot3(xv, mine, NT)
    pack(part, pvec, send0)
    scatter0.start()
    a01_out[...] = a01[...]
    scatter0.wait_recv()
    mid0[...] = send0[sub] + jnp.sum(recv0[1:], axis=0)
    across.start()
    across.wait_recv()
    total = mid0[...]
    recvg[0] = total
    order = [recvg[lax.rem(grp - g + ngrp, ngrp)] for g in range(ngrp)]
    total = order[0]
    for g in range(1, ngrp):
        total = total + order[g]
    all0[sub] = total
    gather0.start()
    gather0.wait_recv()
    unpack(all0, a0_out, b0_out)
    for exchange in (scatter1, gather1, scatter01, gather01, scatter0, across, gather0):
        exchange.wait_send()


def root_kernel(prior, a0, b0, inv1, a01, a1, xneg, basis, root, group, fine, field, mat):
    mat[...] = prior[...] + a0[...]
    negative_inverse(mat)
    mean0 = -row_dot(b0[0:1, :], mat[...])
    root[...] = mean0
    mean1 = -row_dot(a1[0:1, :] - row_dot(mean0, a01[...]), inv1[...])
    group[...] = mean1
    mean2 = row_dot(mean1, xneg[0:R, :]) + row_dot(mean0, xneg[R : 2 * R, :]) - xneg[2 * R : 2 * R + 1, :]
    fine[...] = mean2

    def fit(mean, a):
        left = jnp.broadcast_to(mean, (16, R)).astype(BF)
        return dot(left, basis[a], NT)

    field[...] = (fit(mean0, 0) + fit(mean1, 1) + fit(mean2, 2))[0:1, :]


def shape(*dims):
    return jax.ShapeDtypeStruct(dims, F32)


PARAMS = dict(vmem_limit_bytes=56 << 20)


def shards(basis, observations, counts, noise_prec, prior_fine, prior_group, prior_root):
    slots = basis.shape[1]
    s11, g01, g00, svec, cross, xneg = pl.pallas_call(
        fine_kernel,
        name="fine",
        out_shape=[shape(R, R), shape(R, R), shape(R, R), shape(32, R), shape(2 * R + 16, R), shape(2 * R + 16, R)],
        in_specs=[SM, SM, VM, VM, VM],
        out_specs=[VM] * 6,
        scratch_shapes=[pltpu.VMEM((R, R), F32)],
        compiler_params=pltpu.CompilerParams(**PARAMS),
    )(counts, noise_prec, basis, observations.reshape(1, slots), prior_fine)
    nsub, ngrp = lax.axis_size("sub"), lax.axis_size("grp")

    def buf(*dims):
        return pltpu.VMEM(dims, F32)

    inv1, a01, a1, a0, b0 = pl.pallas_call(
        group_kernel,
        name="group",
        out_shape=[shape(R, R), shape(R, R), shape(8, R), shape(R, R), shape(8, R)],
        in_specs=[VM] * 7,
        out_specs=[VM] * 5,
        scratch_shapes=[
            buf(nsub, PIECE, 128), buf(nsub, PIECE, 128), buf(nsub, PIECE, 128),
            buf(R, R), buf(nsub, R // nsub, R), buf(R, R),
            buf(R, R), buf(16, R),
            buf(nsub, PIECE, 128), buf(nsub, PIECE, 128), buf(PIECE, 128), buf(ngrp, PIECE, 128), buf(nsub, PIECE, 128),
            pltpu.SemaphoreType.DMA((6, nsub)), pltpu.SemaphoreType.DMA((6, nsub)),
            pltpu.SemaphoreType.DMA((ngrp,)), pltpu.SemaphoreType.DMA((ngrp,)),
        ],
        compiler_params=pltpu.CompilerParams(collective_id=0, has_side_effects=True, **PARAMS),
    )(prior_group, s11, g01, g00, svec, cross, xneg)
    root, group, fine, field = pl.pallas_call(
        root_kernel,
        name="root",
        out_shape=[shape(1, R), shape(1, R), shape(1, R), shape(1, slots)],
        in_specs=[VM] * 8,
        out_specs=[VM] * 4,
        scratch_shapes=[pltpu.VMEM((R, R), F32)],
        compiler_params=pltpu.CompilerParams(**PARAMS),
    )(prior_root, a0, b0, inv1, a01, a1, xneg, basis)
    piece = R // lax.axis_size("sub")
    position = lax.axis_index("sub") * piece
    return (
        lax.dynamic_slice_in_dim(root[0], position, piece),
        lax.dynamic_slice_in_dim(group[0], position, piece),
        fine[0],
        field[0],
    )


def solution(mesh):
    in_specs = (
        P(None, ("grp", "sub"), None),
        P(("grp", "sub")),
        P(("grp", "sub")),
        P(("grp", "sub")),
        P(("grp", "sub"), None, None),
        P("grp", None, None),
        P(),
    )
    out_specs = (P("sub"), P(("grp", "sub")), P(("grp", "sub")), P(("grp", "sub")))
    return jax.shard_map(shards, mesh=mesh, in_specs=in_specs, out_specs=out_specs, check_vma=False)
```

```python
import functools

import jax
import jax.numpy as jnp
from jax import lax
from jax.experimental import pallas as pl
from jax.experimental.pallas import tpu as pltpu
from jax.sharding import PartitionSpec as P

F32 = jnp.float32
BF = jnp.bfloat16
MESH = pl.DeviceIdType.MESH
R = 512
NB = 16
CUTS = (8, 24)
VM = pl.BlockSpec(memory_space=pltpu.VMEM)
SM = pl.BlockSpec(memory_space=pltpu.SMEM)
HB = pl.BlockSpec(memory_space=pl.ANY)
NN = (((1,), (0,)), ((), ()))
TN = (((0,), (0,)), ((), ()))
NT = (((1,), (1,)), ((), ()))


def split2(x):
    high = x.astype(BF)
    return high, (x - high.astype(F32)).astype(BF)


def split3(x):
    high = x.astype(BF)
    rest = x - high.astype(F32)
    mid = rest.astype(BF)
    return high, mid, (rest - mid.astype(F32)).astype(BF)


def dot(left, right, dims):
    return lax.dot_general(left, right, dims, preferred_element_type=F32)


def dot3(left, right, dims):
    a, b = left if isinstance(left, tuple) else split2(left)
    c, d = right if isinstance(right, tuple) else split2(right)
    return dot(a, c, dims) + (dot(a, d, dims) + dot(b, c, dims))


def rank_update(rows, panel):
    a, b, c = split3(rows)
    d, e, f = split3(panel)
    return dot(jnp.concatenate([a, a, b, a, b, c], 0), jnp.concatenate([d, e, d, f, e, d], 0), TN)


def sweep_panel(mat, p):
    tiles = mat.shape[1] // 128
    row0 = pl.multiple_of(p * NB, NB)
    tile = lax.div(p * NB, 128)
    lane0 = pl.multiple_of(tile * 128, 128)
    first = p * NB - tile * 128
    rows = mat[pl.ds(row0, NB), :]
    diag = mat[pl.ds(row0, NB), pl.ds(lane0, 128)]
    sub = lax.broadcasted_iota(jnp.int32, (NB, 128), 0)
    lane = lax.broadcasted_iota(jnp.int32, (NB, 128), 1)
    cols = []
    for j in range(NB):
        col = jnp.sum(jnp.where(lane == first + j, diag, 0.0), axis=1, keepdims=True)
        cols.append(jnp.broadcast_to(col, (NB, 128)))
    inside = (lane >= first) & (lane < first + NB)
    eye = jnp.where(lane == first + sub, -1.0, 0.0)
    blocks = [jnp.where(inside & (tile == c), eye, rows[:, c * 128 : c * 128 + 128]) for c in range(tiles)]
    work = jnp.stack(cols + blocks, 0)
    for i in range(NB):
        inv = 1.0 / jnp.broadcast_to(work[0, i : i + 1, :], (NB, 128))
        mult = jnp.where(sub == i, inv, -work[0] * inv)
        work = work[1:]
        pivot_row = jnp.broadcast_to(work[:, i : i + 1, :], work.shape)
        work = jnp.where((sub == i)[None], 0.0, work) + mult[None] * pivot_row
    panel = jnp.concatenate([work[c] for c in range(tiles)], 1)
    lane1 = lax.broadcasted_iota(jnp.int32, (1, 128), 1)
    mask = (lane1 >= first) & (lane1 < first + NB)
    mat[:, pl.ds(lane0, 128)] = jnp.where(mask, 0.0, mat[:, pl.ds(lane0, 128)])
    mat[...] = mat[...] - rank_update(rows, panel)
    mat[pl.ds(row0, NB), :] = panel


def sweep_panels(mat, low, high):
    def body(p, carry):
        sweep_panel(mat, p)
        return carry

    lax.fori_loop(low, high, body, 0)


def negative_inverse(mat):
    sweep_panels(mat, 0, mat.shape[0] // NB)


def row_dot(vec, parts):
    a, b, c = [part.astype(F32) for part in split3(vec)]
    index = lax.broadcasted_iota(jnp.int32, (16, vec.shape[1]), 0)
    left = jnp.where(index == 0, a, jnp.where(index == 1, b, jnp.where(index == 2, c, 0.0))).astype(BF)
    out = dot(left, parts[0], NN) + dot(left, parts[1], NN)
    return jnp.sum(out, axis=0, keepdims=True)


SLAB = 16
TILES = R // 128
SYM = 5 * SLAB
PIECE = SYM + 8
HALF = 8


def piece_tiles(group):
    low = group + 1
    return [(False, t) for t in range(low)] + [(True, t) for t in range(5 - low)]


def slab_rows(index):
    return pl.ds(pl.multiple_of(index * SLAB, SLAB), SLAB)


def pack(full, vec, pieces):
    pieces[:, SYM:PIECE, :] = jnp.zeros((pieces.shape[0], 8, 128), F32)
    for group in range(2):

        def body(i, carry):
            s = group * HALF + i
            for t, (high, tile) in enumerate(piece_tiles(group)):
                rows = slab_rows(2 * pieces.shape[0] - 1 - s if high else s)
                pieces[s, SLAB * t : SLAB * t + SLAB, :] = full[rows, 128 * tile : 128 * tile + 128]
            return carry

        lax.fori_loop(0, HALF, body, 0)
    for c in range(TILES):
        pieces[4 * c, SYM:PIECE, :] = vec[0:8, 128 * c : 128 * c + 128]


def unpack(pieces, full, vec):
    for group in range(2):

        def body(i, carry):
            s = group * HALF + i
            for t, (high, tile) in enumerate(piece_tiles(group)):
                rows = slab_rows(2 * pieces.shape[0] - 1 - s if high else s)
                full[rows, 128 * tile : 128 * tile + 128] = pieces[s, SLAB * t : SLAB * t + SLAB, :]
            return carry

        lax.fori_loop(0, HALF, body, 0)
    for i in range(TILES):
        for j in range(i):
            full[128 * j : 128 * j + 128, 128 * i : 128 * i + 128] = full[
                128 * i : 128 * i + 128, 128 * j : 128 * j + 128
            ].T
    for c in range(TILES):
        vec[0:8, 128 * c : 128 * c + 128] = pieces[4 * c, SYM:PIECE, :]


class Exchange:
    def __init__(self, axis, source, into, send_sem, recv_sem):
        self.axis, self.source, self.into, self.send_sem, self.recv_sem = axis, source, into, send_sem, recv_sem
        self.n = lax.axis_size(axis)
        self.me = lax.axis_index(axis)

    def copy(self, d):
        peer = lax.rem(self.me + d, self.n)
        return pltpu.make_async_remote_copy(
            src_ref=self.source(peer),
            dst_ref=self.into(d),
            send_sem=self.send_sem.at[d],
            recv_sem=self.recv_sem.at[d],
            device_id={self.axis: peer},
            device_id_type=MESH,
        )

    def each(self, act):
        def body(d, carry):
            act(self.copy(d))
            return carry

        lax.fori_loop(1, self.n, body, 0)

    def start(self):
        self.each(lambda copy: copy.start())

    def wait_recv(self):
        self.each(lambda copy: copy.wait_recv())

    def wait_send(self):
        self.each(lambda copy: copy.wait_send())


def first_row(vec, rows):
    total = jnp.sum(vec, axis=0, keepdims=True)
    index = lax.broadcasted_iota(jnp.int32, (rows, vec.shape[1]), 0)
    return jnp.where(index == 0, total, 0.0)


def kernel(
    count, tau, obs, basis_hbm, fine_hbm, group_hbm, root_hbm,
    root_out, group_out, fine_out, field_out,
    basis, mat, prior1, prior0, cross, high, low, xvec, s11, s01, s00, vec1, vec0, inv1, a01, a1, b0,
    send1, recv1, all1, recv01, send0, recv0, mid0, recvg, all0,
    load_sem, sem_s, sem_r, semg_s, semg_r,
):
    sub = lax.axis_index("sub")
    grp = lax.axis_index("grp")
    nsub, ngrp = lax.axis_size("sub"), lax.axis_size("grp")
    rows = R // nsub

    def load(k):
        pairs = (
            (basis_hbm.at[2], basis.at[2]), (fine_hbm.at[0], mat), (basis_hbm.at[1], basis.at[1]),
            (basis_hbm.at[0], basis.at[0]), (group_hbm.at[0], prior1), (root_hbm, prior0),
        )
        return pltpu.make_async_copy(pairs[k][0], pairs[k][1], load_sem.at[k])

    for k in range(6):
        load(k).start()
    barrier = pltpu.get_barrier_semaphore()

    def greet(axis, me, n):
        def body(d, carry):
            pl.semaphore_signal(
                barrier, inc=1, device_id={axis: lax.rem(me + d, n)}, device_id_type=MESH
            )
            return carry

        lax.fori_loop(1, n, body, 0)

    greet("sub", sub, nsub)
    greet("grp", grp, ngrp)

    slab = pl.ds(pl.multiple_of(sub * rows, rows), rows)
    scatter1 = Exchange("sub", lambda peer: send1.at[peer], lambda d: recv1.at[d], sem_s.at[0], sem_r.at[0])
    gather1 = Exchange("sub", lambda peer: all1.at[sub], lambda d: all1.at[sub], sem_s.at[1], sem_r.at[1])
    scatter01 = Exchange(
        "sub", lambda peer: s01.at[pl.ds(pl.multiple_of(peer * rows, rows), rows), :], lambda d: recv01.at[d],
        sem_s.at[2], sem_r.at[2],
    )
    gather01 = Exchange("sub", lambda peer: a01.at[slab, :], lambda d: a01.at[slab, :], sem_s.at[3], sem_r.at[3])
    scatter0 = Exchange("sub", lambda peer: send0.at[peer], lambda d: recv0.at[d], sem_s.at[4], sem_r.at[4])
    gather0 = Exchange("sub", lambda peer: all0.at[sub], lambda d: all0.at[sub], sem_s.at[5], sem_r.at[5])
    across = Exchange("grp", lambda peer: mid0, lambda d: recvg.at[d], semg_s, semg_r)

    slots = basis.shape[1]
    t = tau[0]
    n = count[0]
    valid = lax.broadcasted_iota(jnp.int32, (slots, 1), 0) < n
    chunks = slots // 128
    index = lax.broadcasted_iota(jnp.int32, (chunks, 128), 0)
    slot = index * 128 + lax.broadcasted_iota(jnp.int32, (chunks, 128), 1)
    y = jnp.where(slot < n, obs[...].astype(F32), 0.0)
    y = jnp.concatenate([jnp.where(index == c, y, 0.0) for c in range(chunks)], 1).astype(BF)

    def masked(a):
        block = basis[a]
        return jnp.where(valid, block, jnp.zeros_like(block))

    load(0).wait()
    m2 = masked(2)
    load(1).wait()
    mat[...] = mat[...] + t * dot(basis[2], m2, TN)
    cross[2 * R : 2 * R + 16, :] = first_row(t * dot(y, basis[2], NN), 16)
    load(2).wait()
    cross[0:R, :] = t * dot(basis[1], m2, TN)
    m1 = masked(1)
    s11[...] = t * dot(basis[1], m1, TN)
    vec1[...] = first_row(t * dot(y, basis[1], NN), 16)
    negative_inverse(mat)

    inv = split2(mat[...])
    c1 = split2(cross[0:R, :])
    x1 = split2(dot3(c1, inv, NN))
    high[0:R, :], low[0:R, :] = x1
    xy = dot3(cross[2 * R : 2 * R + 16, :], inv, NN)
    xvec[...] = xy
    s11[...] = s11[...] + dot3(x1, c1, NT)
    vec1[...] = vec1[...] + dot3(xy, c1, NT)
    pack(s11, vec1, send1)
    pl.semaphore_wait(barrier, nsub + ngrp - 2)
    scatter1.start()

    load(3).wait()
    m0 = masked(0)
    cross[R : 2 * R, :] = t * dot(m0, basis[2], TN)
    c0 = split2(cross[R : 2 * R, :])
    x0 = split2(dot3(c0, inv, NN))
    high[R : 2 * R, :], low[R : 2 * R, :] = x0
    s01[...] = t * dot(m0, basis[1], TN) + dot3(x0, c1, NT)
    scatter01.start()
    s00[...] = t * dot(m0, basis[0], TN) + dot3(x0, c0, NT)
    vec0[...] = first_row(t * dot(y, basis[0], NN), 16) + dot3(xy, c0, NT)
    pack(s00, vec0, send0)
    scatter1.wait_recv()
    all1[sub] = send1[sub] + jnp.sum(recv1[1:], axis=0)
    gather1.start()
    gather1.wait_recv()
    unpack(all1, inv1, a1)
    load(4).wait()
    inv1[...] = inv1[...] + prior1[...]
    panels = R // NB
    cuts = (panels * CUTS[0] // 32, panels * CUTS[1] // 32)
    sweep_panels(inv1, 0, cuts[0])
    scatter01.wait_recv()
    a01[slab, :] = s01[slab, :] + jnp.sum(recv01[1:], axis=0)
    gather01.start()
    scatter0.start()
    sweep_panels(inv1, cuts[0], cuts[1])
    scatter0.wait_recv()
    mid0[...] = send0[sub] + jnp.sum(recv0[1:], axis=0)
    sweep_panels(inv1, cuts[1], panels)
    gather01.wait_recv()

    inv = split2(inv1[...])
    both = split2(a01[...])
    left = jnp.concatenate(
        [a01[slab_rows(sub), :], a01[slab_rows(2 * nsub - 1 - sub), :], a1[...], jnp.zeros((8, R), F32)], 0
    )
    term = dot3(dot3(left, inv, NN), both, NT)
    upper = sub >= HALF
    for k, (one, two) in enumerate(zip(piece_tiles(0), piece_tiles(1))):
        parts = [
            term[SLAB * hi : SLAB * hi + SLAB, 128 * tile : 128 * tile + 128] for hi, tile in (one, two)
        ]
        place = slice(SLAB * k, SLAB * k + SLAB)
        mid0[place, :] = mid0[place, :] + jnp.where(upper, parts[1], parts[0])
    extra = jnp.zeros((8, 128), F32)
    for c in range(TILES):
        extra = extra + jnp.where(sub == 4 * c, term[2 * SLAB : 2 * SLAB + 8, 128 * c : 128 * c + 128], 0.0)
    mid0[SYM:PIECE, :] = mid0[SYM:PIECE, :] + extra
    across.start()
    across.wait_recv()
    recvg[0] = mid0[...]
    total = recvg[grp]
    for g in range(1, ngrp):
        total = total + recvg[lax.rem(grp - g + ngrp, ngrp)]
    all0[sub] = total
    gather0.start()
    gather0.wait_recv()
    unpack(all0, mat, b0)
    load(5).wait()
    mat[...] = mat[...] + prior0[...]
    negative_inverse(mat)
    mean0 = -row_dot(b0[0:1, :], split2(mat[...]))
    mean1 = -row_dot(a1[0:1, :] - row_dot(mean0, both), inv)
    mean2 = (
        row_dot(mean1, (high[0:R, :], low[0:R, :])) + row_dot(mean0, (high[R : 2 * R, :], low[R : 2 * R, :]))
        - xvec[0:1, :]
    )
    root_out[...] = mean0
    group_out[...] = mean1
    fine_out[...] = mean2

    def fit(mean, a):
        left = jnp.broadcast_to(mean, (16, R)).astype(BF)
        return dot(left, basis[a], NT)

    field_out[...] = (fit(mean0, 0) + fit(mean1, 1) + fit(mean2, 2))[0:1, :]
    for exchange in (scatter1, gather1, scatter01, gather01, scatter0, across, gather0):
        exchange.wait_send()


def shape(*dims):
    return jax.ShapeDtypeStruct(dims, F32)


def shards(basis, observations, counts, noise_prec, prior_fine, prior_group, prior_root):
    slots = basis.shape[1]
    nsub, ngrp = lax.axis_size("sub"), lax.axis_size("grp")

    def buf(*dims, kind=F32):
        return pltpu.VMEM(dims, kind)

    root, group, fine, field = pl.pallas_call(
        kernel,
        name="levels",
        out_shape=[shape(1, R), shape(1, R), shape(1, R), shape(1, slots)],
        in_specs=[SM, SM, VM, HB, HB, HB, HB],
        out_specs=[VM] * 4,
        scratch_shapes=[
            buf(3, slots, R, kind=BF), buf(R, R), buf(R, R), buf(R, R), buf(2 * R + 16, R),
            buf(2 * R, R, kind=BF), buf(2 * R, R, kind=BF), buf(16, R),
            buf(R, R), buf(R, R), buf(R, R), buf(16, R), buf(16, R), buf(R, R), buf(R, R), buf(8, R), buf(8, R),
            buf(nsub, PIECE, 128), buf(nsub, PIECE, 128), buf(nsub, PIECE, 128), buf(nsub, R // nsub, R),
            buf(nsub, PIECE, 128), buf(nsub, PIECE, 128), buf(PIECE, 128), buf(ngrp, PIECE, 128), buf(nsub, PIECE, 128),
            pltpu.SemaphoreType.DMA((6,)),
            pltpu.SemaphoreType.DMA((6, nsub)), pltpu.SemaphoreType.DMA((6, nsub)),
            pltpu.SemaphoreType.DMA((ngrp,)), pltpu.SemaphoreType.DMA((ngrp,)),
        ],
        compiler_params=pltpu.CompilerParams(collective_id=0, has_side_effects=True, vmem_limit_bytes=60 << 20),
    )(counts, noise_prec, observations.reshape(slots // 128, 128), basis, prior_fine, prior_group, prior_root)
    piece = R // lax.axis_size("sub")
    position = lax.axis_index("sub") * piece
    return (
        lax.dynamic_slice_in_dim(root[0], position, piece),
        lax.dynamic_slice_in_dim(group[0], position, piece),
        fine[0],
        field[0],
    )


def solution(mesh):
    in_specs = (
        P(None, ("grp", "sub"), None),
        P(("grp", "sub")),
        P(("grp", "sub")),
        P(("grp", "sub")),
        P(("grp", "sub"), None, None),
        P("grp", None, None),
        P(),
    )
    out_specs = (P("sub"), P(("grp", "sub")), P(("grp", "sub")), P(("grp", "sub")))
    return jax.shard_map(shards, mesh=mesh, in_specs=in_specs, out_specs=out_specs, check_vma=False)
```

```python
import functools

import jax
import jax.numpy as jnp
from jax import lax
from jax.experimental import pallas as pl
from jax.experimental.pallas import tpu as pltpu
from jax.sharding import PartitionSpec as P

F32 = jnp.float32
BF = jnp.bfloat16
MESH = pl.DeviceIdType.MESH
R = 512
NB = 16
CUTS = (6, 14, 22)
VM = pl.BlockSpec(memory_space=pltpu.VMEM)
SM = pl.BlockSpec(memory_space=pltpu.SMEM)
HB = pl.BlockSpec(memory_space=pl.ANY)
NN = (((1,), (0,)), ((), ()))
TN = (((0,), (0,)), ((), ()))
NT = (((1,), (1,)), ((), ()))


def split2(x):
    high = x.astype(BF)
    return high, (x - high.astype(F32)).astype(BF)


def split3(x):
    high = x.astype(BF)
    rest = x - high.astype(F32)
    mid = rest.astype(BF)
    return high, mid, (rest - mid.astype(F32)).astype(BF)


def dot(left, right, dims):
    return lax.dot_general(left, right, dims, preferred_element_type=F32)


def dot3(left, right, dims):
    a, b = left if isinstance(left, tuple) else split2(left)
    c, d = right if isinstance(right, tuple) else split2(right)
    return dot(a, c, dims) + (dot(a, d, dims) + dot(b, c, dims))


def rank_update(rows, panel):
    a, b, c = split3(rows)
    d, e, f = split3(panel)
    return dot(jnp.concatenate([a, a, b, a, b, c], 0), jnp.concatenate([d, e, d, f, e, d], 0), TN)


def sweep_panel(mat, p):
    tiles = mat.shape[1] // 128
    row0 = pl.multiple_of(p * NB, NB)
    tile = lax.div(p * NB, 128)
    lane0 = pl.multiple_of(tile * 128, 128)
    first = p * NB - tile * 128
    rows = mat[pl.ds(row0, NB), :]
    diag = mat[pl.ds(row0, NB), pl.ds(lane0, 128)]
    sub = lax.broadcasted_iota(jnp.int32, (NB, 128), 0)
    lane = lax.broadcasted_iota(jnp.int32, (NB, 128), 1)
    cols = []
    for j in range(NB):
        col = jnp.sum(jnp.where(lane == first + j, diag, 0.0), axis=1, keepdims=True)
        cols.append(jnp.broadcast_to(col, (NB, 128)))
    inside = (lane >= first) & (lane < first + NB)
    eye = jnp.where(lane == first + sub, -1.0, 0.0)
    blocks = [jnp.where(inside & (tile == c), eye, rows[:, c * 128 : c * 128 + 128]) for c in range(tiles)]
    work = jnp.stack(cols + blocks, 0)
    for i in range(NB):
        inv = 1.0 / jnp.broadcast_to(work[0, i : i + 1, :], (NB, 128))
        mult = jnp.where(sub == i, inv, -work[0] * inv)
        work = work[1:]
        pivot_row = jnp.broadcast_to(work[:, i : i + 1, :], work.shape)
        work = jnp.where((sub == i)[None], 0.0, work) + mult[None] * pivot_row
    panel = jnp.concatenate([work[c] for c in range(tiles)], 1)
    lane1 = lax.broadcasted_iota(jnp.int32, (1, 128), 1)
    mask = (lane1 >= first) & (lane1 < first + NB)
    mat[:, pl.ds(lane0, 128)] = jnp.where(mask, 0.0, mat[:, pl.ds(lane0, 128)])
    mat[...] = mat[...] - rank_update(rows, panel)
    mat[pl.ds(row0, NB), :] = panel


def sweep_panels(mat, low, high):
    def body(p, carry):
        sweep_panel(mat, p)
        return carry

    lax.fori_loop(low, high, body, 0)


def negative_inverse(mat):
    sweep_panels(mat, 0, mat.shape[0] // NB)


def row_dot(vec, parts):
    a, b, c = [part.astype(F32) for part in split3(vec)]
    index = lax.broadcasted_iota(jnp.int32, (16, vec.shape[1]), 0)
    left = jnp.where(index == 0, a, jnp.where(index == 1, b, jnp.where(index == 2, c, 0.0))).astype(BF)
    out = dot(left, parts[0], NN) + dot(left, parts[1], NN)
    return jnp.sum(out, axis=0, keepdims=True)


SLAB = 16
TILES = R // 128
SYM = 5 * SLAB
PIECE = SYM + 8
CUT = 48
HALF = 8
SIDE = 4


def piece_tiles(group):
    low = group + 1
    return [(False, t) for t in range(low)] + [(True, t) for t in range(5 - low)]


def slab_rows(index):
    return pl.ds(pl.multiple_of(index * SLAB, SLAB), SLAB)


def pack(full, vec, pieces):
    pieces[:, :, SYM:PIECE, :] = jnp.zeros((SIDE, SIDE, 8, 128), F32)
    for group in range(2):

        def body(i, carry):
            s = group * HALF + i
            for t, (high, tile) in enumerate(piece_tiles(group)):
                rows = slab_rows(2 * SIDE * SIDE - 1 - s if high else s)
                pieces[lax.div(s, SIDE), lax.rem(s, SIDE), SLAB * t : SLAB * t + SLAB, :] = full[
                    rows, 128 * tile : 128 * tile + 128
                ]
            return carry

        lax.fori_loop(0, HALF, body, 0)
    for c in range(TILES):
        pieces[c, 0, SYM:PIECE, :] = vec[0:8, 128 * c : 128 * c + 128]


def unpack(pieces, full, vec):
    for group in range(2):

        def body(i, carry):
            s = group * HALF + i
            for t, (high, tile) in enumerate(piece_tiles(group)):
                rows = slab_rows(2 * SIDE * SIDE - 1 - s if high else s)
                full[rows, 128 * tile : 128 * tile + 128] = pieces[
                    lax.div(s, SIDE), lax.rem(s, SIDE), SLAB * t : SLAB * t + SLAB, :
                ]
            return carry

        lax.fori_loop(0, HALF, body, 0)
    for i in range(TILES):
        for j in range(i):
            full[128 * j : 128 * j + 128, 128 * i : 128 * i + 128] = full[
                128 * i : 128 * i + 128, 128 * j : 128 * j + 128
            ].T
    for c in range(TILES):
        vec[0:8, 128 * c : 128 * c + 128] = pieces[c, 0, SYM:PIECE, :]


class Exchange:
    def __init__(self, axis, source, into, send_sem, recv_sem):
        self.axis, self.source, self.into, self.send_sem, self.recv_sem = axis, source, into, send_sem, recv_sem
        self.n = lax.axis_size(axis)
        self.me = lax.axis_index(axis)

    def copy(self, d):
        peer = lax.rem(self.me + d, self.n)
        return pltpu.make_async_remote_copy(
            src_ref=self.source(peer),
            dst_ref=self.into(d),
            send_sem=self.send_sem.at[d],
            recv_sem=self.recv_sem.at[d],
            device_id={self.axis: peer},
            device_id_type=MESH,
        )

    def each(self, act):
        def body(d, carry):
            act(self.copy(d))
            return carry

        lax.fori_loop(1, self.n, body, 0)

    def start(self):
        self.each(lambda copy: copy.start())

    def wait_recv(self):
        self.each(lambda copy: copy.wait_recv())

    def wait_send(self):
        self.each(lambda copy: copy.wait_send())


class Grid:
    def __init__(self, source, cut, from_x, from_y, mid_x, mid_y, late_x, late_y, result, send_sem, recv_sem):
        self.source, self.cut, self.result = source, cut, result
        self.from_x, self.from_y, self.mid_x, self.mid_y = from_x, from_y, mid_x, mid_y
        self.late_x, self.late_y = late_x, late_y
        self.send_sem, self.recv_sem = send_sem, recv_sem
        sub = lax.axis_index("sub")
        self.px, self.py = lax.div(sub, SIDE), lax.rem(sub, SIDE)
        self.first, self.rest = slice(0, cut), slice(cut, source.shape[2])

    def copies(self, phase):
        out = []
        px, py, first, rest = self.px, self.py, self.first, self.rest
        source, result = self.source, self.result
        for d in range(1, SIDE):
            x, y = lax.rem(px + d, SIDE), lax.rem(py + d, SIDE)
            at_x, at_y = x * SIDE + py, px * SIDE + y
            if phase == 0:
                pair = (
                    (source.at[x, :, first, :], self.from_x.at[d], at_x),
                    (source.at[:, y, rest, :], self.from_y.at[d], at_y),
                )
            elif phase == 1:
                pair = (
                    (self.mid_x.at[y], self.late_x.at[d], at_y),
                    (self.mid_y.at[x], self.late_y.at[d], at_x),
                )
            elif phase == 2:
                one, two = result.at[px, py, first, :], result.at[px, py, rest, :]
                pair = ((one, one, at_y), (two, two, at_x))
            else:
                one, two = result.at[px, :, first, :], result.at[:, py, rest, :]
                pair = ((one, one, at_x), (two, two, at_y))
            for k, (src, dst, peer) in enumerate(pair):
                out.append(
                    pltpu.make_async_remote_copy(
                        src_ref=src,
                        dst_ref=dst,
                        send_sem=self.send_sem.at[phase, k, d],
                        recv_sem=self.recv_sem.at[phase, k, d],
                        device_id={"sub": peer},
                        device_id_type=MESH,
                    )
                )
        return out

    def start(self, phase):
        for copy in self.copies(phase):
            copy.start()

    def wait_recv(self, phase):
        for copy in self.copies(phase):
            copy.wait_recv()

    def wait_send(self, phases):
        for phase in phases:
            for copy in self.copies(phase):
                copy.wait_send()

    def middle(self):
        self.mid_x[...] = self.source[self.px, :, self.first, :] + jnp.sum(self.from_x[1:], axis=0)
        self.mid_y[...] = self.source[:, self.py, self.rest, :] + jnp.sum(self.from_y[1:], axis=0)

    def finish(self, target):
        target[self.first, :] = self.mid_x[self.py] + jnp.sum(self.late_x[1:], axis=0)
        target[self.rest, :] = self.mid_y[self.px] + jnp.sum(self.late_y[1:], axis=0)


def first_row(vec, rows):
    total = jnp.sum(vec, axis=0, keepdims=True)
    index = lax.broadcasted_iota(jnp.int32, (rows, vec.shape[1]), 0)
    return jnp.where(index == 0, total, 0.0)


def kernel(
    count, tau, obs, basis_hbm, fine_hbm, group_hbm, root_hbm,
    root_out, group_out, fine_out, field_out,
    basis, mat, prior1, prior0, cross, high, low, xvec, s11, s01, s00, vec1, vec0, inv1, a01, a1, b0,
    mid0, recvg, all0, bufs1, bufs01, bufs0, load_sem, sem_s, sem_r, sema_s, sema_r, semg_s, semg_r,
):
    sub = lax.axis_index("sub")
    grp = lax.axis_index("grp")
    nsub, ngrp = lax.axis_size("sub"), lax.axis_size("grp")
    rows = R // nsub

    def load(k):
        pairs = (
            (basis_hbm.at[2], basis.at[2]), (fine_hbm.at[0], mat), (basis_hbm.at[1], basis.at[1]),
            (basis_hbm.at[0], basis.at[0]), (group_hbm.at[0], prior1), (root_hbm, prior0),
        )
        return pltpu.make_async_copy(pairs[k][0], pairs[k][1], load_sem.at[k])

    for k in range(6):
        load(k).start()
    barrier = pltpu.get_barrier_semaphore()

    def greet(axis, me, n):
        def body(d, carry):
            pl.semaphore_signal(
                barrier, inc=1, device_id={axis: lax.rem(me + d, n)}, device_id_type=MESH
            )
            return carry

        lax.fori_loop(1, n, body, 0)

    greet("sub", sub, nsub)
    greet("grp", grp, ngrp)

    px, py = lax.div(sub, SIDE), lax.rem(sub, SIDE)
    send1, all1 = bufs1[0], bufs1[7]
    grid1 = Grid(send1, CUT, *bufs1[1:], sem_s.at[0], sem_r.at[0])
    grid01 = Grid(s01, rows // 2, *bufs01, a01, sem_s.at[1], sem_r.at[1])
    send0 = bufs0[0]
    grid0 = Grid(send0, CUT, *bufs0[1:], None, sem_s.at[2], sem_r.at[2])
    gather0 = Exchange("sub", lambda peer: all0.at[px, py], lambda d: all0.at[px, py], sema_s, sema_r)
    across = Exchange("grp", lambda peer: mid0, lambda d: recvg.at[d], semg_s, semg_r)

    slots = basis.shape[1]
    t = tau[0]
    n = count[0]
    valid = lax.broadcasted_iota(jnp.int32, (slots, 1), 0) < n
    chunks = slots // 128
    index = lax.broadcasted_iota(jnp.int32, (chunks, 128), 0)
    slot = index * 128 + lax.broadcasted_iota(jnp.int32, (chunks, 128), 1)
    y = jnp.where(slot < n, obs[...].astype(F32), 0.0)
    y = jnp.concatenate([jnp.where(index == c, y, 0.0) for c in range(chunks)], 1).astype(BF)

    def masked(a):
        block = basis[a]
        return jnp.where(valid, block, jnp.zeros_like(block))

    load(0).wait()
    m2 = masked(2)
    load(1).wait()
    mat[...] = mat[...] + t * dot(basis[2], m2, TN)
    cross[2 * R : 2 * R + 16, :] = first_row(t * dot(y, basis[2], NN), 16)
    load(2).wait()
    cross[0:R, :] = t * dot(basis[1], m2, TN)
    m1 = masked(1)
    s11[...] = t * dot(basis[1], m1, TN)
    vec1[...] = first_row(t * dot(y, basis[1], NN), 16)
    negative_inverse(mat)

    inv = split2(mat[...])
    c1 = split2(cross[0:R, :])
    x1 = split2(dot3(c1, inv, NN))
    high[0:R, :], low[0:R, :] = x1
    xy = dot3(cross[2 * R : 2 * R + 16, :], inv, NN)
    xvec[...] = xy
    s11[...] = s11[...] + dot3(x1, c1, NT)
    vec1[...] = vec1[...] + dot3(xy, c1, NT)
    pack(s11, vec1, send1)
    pl.semaphore_wait(barrier, nsub + ngrp - 2)
    grid1.start(0)

    load(3).wait()
    m0 = masked(0)
    cross[R : 2 * R, :] = t * dot(m0, basis[2], TN)
    c0 = split2(cross[R : 2 * R, :])
    x0 = split2(dot3(c0, inv, NN))
    high[R : 2 * R, :], low[R : 2 * R, :] = x0
    s01[...] = (t * dot(m0, basis[1], TN) + dot3(x0, c1, NT)).reshape(SIDE, SIDE, rows, R)
    grid01.start(0)
    grid1.wait_recv(0)
    grid1.middle()
    grid1.start(1)
    s00[...] = t * dot(m0, basis[0], TN) + dot3(x0, c0, NT)
    vec0[...] = first_row(t * dot(y, basis[0], NN), 16) + dot3(xy, c0, NT)
    pack(s00, vec0, send0)
    grid1.wait_recv(1)
    grid1.finish(all1.at[px, py])
    grid1.start(2)
    grid01.wait_recv(0)
    grid01.middle()
    grid01.start(1)
    grid1.wait_recv(2)
    grid1.start(3)
    grid01.wait_recv(1)
    grid01.finish(a01.at[px, py])
    grid01.start(2)
    grid1.wait_recv(3)
    unpack(all1, inv1, a1)
    load(4).wait()
    inv1[...] = inv1[...] + prior1[...]
    panels = R // NB
    cuts = [panels * c // 32 for c in CUTS]
    sweep_panels(inv1, 0, cuts[0])
    grid01.wait_recv(2)
    grid01.start(3)
    grid0.start(0)
    sweep_panels(inv1, cuts[0], cuts[1])
    grid0.wait_recv(0)
    grid0.middle()
    grid0.start(1)
    sweep_panels(inv1, cuts[1], cuts[2])
    grid0.wait_recv(1)
    grid0.finish(mid0)
    sweep_panels(inv1, cuts[2], panels)
    grid01.wait_recv(3)

    inv = split2(inv1[...])
    both = split2(a01[...].reshape(R, R))
    mine, mirror = lax.div(sub, 2), lax.div(2 * nsub - 1 - sub, 2)
    half = pl.multiple_of(lax.rem(sub, 2) * SLAB, SLAB)
    left = jnp.concatenate(
        [
            a01[lax.div(mine, SIDE), lax.rem(mine, SIDE), pl.ds(half, SLAB), :],
            a01[lax.div(mirror, SIDE), lax.rem(mirror, SIDE), pl.ds(pl.multiple_of(SLAB - half, SLAB), SLAB), :],
            a1[...], jnp.zeros((8, R), F32),
        ],
        0,
    )
    term = dot3(dot3(left, inv, NN), both, NT)
    upper = sub >= HALF
    for k, (one, two) in enumerate(zip(piece_tiles(0), piece_tiles(1))):
        parts = [
            term[SLAB * hi : SLAB * hi + SLAB, 128 * tile : 128 * tile + 128] for hi, tile in (one, two)
        ]
        place = slice(SLAB * k, SLAB * k + SLAB)
        mid0[place, :] = mid0[place, :] + jnp.where(upper, parts[1], parts[0])
    extra = jnp.zeros((8, 128), F32)
    for c in range(TILES):
        extra = extra + jnp.where(sub == 4 * c, term[2 * SLAB : 2 * SLAB + 8, 128 * c : 128 * c + 128], 0.0)
    mid0[SYM:PIECE, :] = mid0[SYM:PIECE, :] + extra
    across.start()
    across.wait_recv()
    recvg[0] = mid0[...]
    total = recvg[grp]
    for g in range(1, ngrp):
        total = total + recvg[lax.rem(grp - g + ngrp, ngrp)]
    all0[px, py] = total
    gather0.start()
    gather0.wait_recv()
    unpack(all0, mat, b0)
    load(5).wait()
    mat[...] = mat[...] + prior0[...]
    negative_inverse(mat)
    mean0 = -row_dot(b0[0:1, :], split2(mat[...]))
    mean1 = -row_dot(a1[0:1, :] - row_dot(mean0, both), inv)
    mean2 = (
        row_dot(mean1, (high[0:R, :], low[0:R, :])) + row_dot(mean0, (high[R : 2 * R, :], low[R : 2 * R, :]))
        - xvec[0:1, :]
    )
    root_out[...] = mean0
    group_out[...] = mean1
    fine_out[...] = mean2

    def fit(mean, a):
        left = jnp.broadcast_to(mean, (16, R)).astype(BF)
        return dot(left, basis[a], NT)

    field_out[...] = (fit(mean0, 0) + fit(mean1, 1) + fit(mean2, 2))[0:1, :]
    grid1.wait_send(range(4))
    grid01.wait_send(range(4))
    grid0.wait_send(range(2))
    across.wait_send()
    gather0.wait_send()


def shape(*dims):
    return jax.ShapeDtypeStruct(dims, F32)


def shards(basis, observations, counts, noise_prec, prior_fine, prior_group, prior_root):
    slots = basis.shape[1]
    nsub, ngrp = lax.axis_size("sub"), lax.axis_size("grp")

    def buf(*dims, kind=F32):
        return pltpu.VMEM(dims, kind)

    def halves(one, two, lanes):
        sizes = (one, two)
        return (
            [buf(SIDE, SIDE, size, lanes) for size in sizes] + [buf(SIDE, size, lanes) for size in sizes]
            + [buf(SIDE, size, lanes) for size in sizes]
        )

    root, group, fine, field = pl.pallas_call(
        kernel,
        name="levels",
        out_shape=[shape(1, R), shape(1, R), shape(1, R), shape(1, slots)],
        in_specs=[SM, SM, VM, HB, HB, HB, HB],
        out_specs=[VM] * 4,
        scratch_shapes=[
            buf(3, slots, R, kind=BF), buf(R, R), buf(R, R), buf(R, R), buf(2 * R + 16, R),
            buf(2 * R, R, kind=BF), buf(2 * R, R, kind=BF), buf(16, R),
            buf(R, R), buf(SIDE, SIDE, R // nsub, R), buf(R, R), buf(16, R), buf(16, R),
            buf(R, R), buf(SIDE, SIDE, R // nsub, R), buf(8, R), buf(8, R),
            buf(PIECE, 128), buf(ngrp, PIECE, 128), buf(SIDE, SIDE, PIECE, 128),
            [buf(SIDE, SIDE, PIECE, 128), *halves(CUT, PIECE - CUT, 128), buf(SIDE, SIDE, PIECE, 128)],
            halves(R // nsub // 2, R // nsub // 2, R),
            [buf(SIDE, SIDE, PIECE, 128), *halves(CUT, PIECE - CUT, 128)],
            pltpu.SemaphoreType.DMA((6,)),
            pltpu.SemaphoreType.DMA((3, 4, 2, SIDE)), pltpu.SemaphoreType.DMA((3, 4, 2, SIDE)),
            pltpu.SemaphoreType.DMA((nsub,)), pltpu.SemaphoreType.DMA((nsub,)),
            pltpu.SemaphoreType.DMA((ngrp,)), pltpu.SemaphoreType.DMA((ngrp,)),
        ],
        compiler_params=pltpu.CompilerParams(collective_id=0, has_side_effects=True, vmem_limit_bytes=60 << 20),
    )(counts, noise_prec, observations.reshape(slots // 128, 128), basis, prior_fine, prior_group, prior_root)
    piece = R // lax.axis_size("sub")
    position = lax.axis_index("sub") * piece
    return (
        lax.dynamic_slice_in_dim(root[0], position, piece),
        lax.dynamic_slice_in_dim(group[0], position, piece),
        fine[0],
        field[0],
    )


def solution(mesh):
    in_specs = (
        P(None, ("grp", "sub"), None),
        P(("grp", "sub")),
        P(("grp", "sub")),
        P(("grp", "sub")),
        P(("grp", "sub"), None, None),
        P("grp", None, None),
        P(),
    )
    out_specs = (P("sub"), P(("grp", "sub")), P(("grp", "sub")), P(("grp", "sub")))
    return jax.shard_map(shards, mesh=mesh, in_specs=in_specs, out_specs=out_specs, check_vma=False)
```

```python
import functools

import jax
import jax.numpy as jnp
from jax import lax
from jax.experimental import pallas as pl
from jax.experimental.pallas import tpu as pltpu
from jax.sharding import PartitionSpec as P

F32 = jnp.float32
BF = jnp.bfloat16
MESH = pl.DeviceIdType.MESH
R = 512
NB = 16
VM = pl.BlockSpec(memory_space=pltpu.VMEM)
SM = pl.BlockSpec(memory_space=pltpu.SMEM)
HB = pl.BlockSpec(memory_space=pl.ANY)
NN = (((1,), (0,)), ((), ()))
TN = (((0,), (0,)), ((), ()))
NT = (((1,), (1,)), ((), ()))


def split2(x):
    high = x.astype(BF)
    return high, (x - high.astype(F32)).astype(BF)


def split3(x):
    high = x.astype(BF)
    rest = x - high.astype(F32)
    mid = rest.astype(BF)
    return high, mid, (rest - mid.astype(F32)).astype(BF)


def dot(left, right, dims):
    return lax.dot_general(left, right, dims, preferred_element_type=F32)


def dot3(left, right, dims):
    a, b = left if isinstance(left, tuple) else split2(left)
    c, d = right if isinstance(right, tuple) else split2(right)
    (k,), (m,) = dims[0]
    return dot(jnp.concatenate([a, a, b], k), jnp.concatenate([c, d, c], m), dims)


def sweep_panel(mat, p):
    first = p * NB
    place = pl.ds(pl.multiple_of(first, NB), NB)
    rows = mat[place, :]
    sub = lax.broadcasted_iota(jnp.int32, (NB, 128), 0)
    lane = lax.broadcasted_iota(jnp.int32, (NB, 128), 1)
    cols = []
    for j in range(NB):
        col = jnp.sum(jnp.where(lane == first + j, rows, 0.0), axis=1, keepdims=True)
        cols.append(jnp.broadcast_to(col, (NB, 128)))
    inside = (lane >= first) & (lane < first + NB)
    eye = jnp.where(lane == first + sub, -1.0, 0.0)
    work = jnp.stack(cols + [jnp.where(inside, eye, rows)], 0)
    for i in range(NB):
        inv = 1.0 / jnp.broadcast_to(work[0, i : i + 1, :], (NB, 128))
        mult = jnp.where(sub == i, inv, -work[0] * inv)
        work = work[1:]
        pivot_row = jnp.broadcast_to(work[:, i : i + 1, :], work.shape)
        work = jnp.where((sub == i)[None], 0.0, work) + mult[None] * pivot_row
    panel = work[0]
    mat[...] = jnp.where(inside[0:1], 0.0, mat[...]) - dot3(rows, panel, TN)
    mat[place, :] = panel


def negative_inverse(mat, block, inner=(), outer=()):
    n = mat.shape[0]

    def body(p, carry):
        sweep_panel(block, p)
        return carry

    for k in range(n // 128):
        mine = slice(128 * k, 128 * k + 128)
        block[...] = mat[mine, mine]
        lax.fori_loop(0, 128 // NB, body, 0)
        if k in dict(inner):
            dict(inner)[k]()
        own = block[...]
        rows = split2(mat[mine, :])
        panel = -dot3(own, rows, NN)
        panel = jnp.concatenate(
            [own if c == k else panel[:, 128 * c : 128 * c + 128] for c in range(n // 128)], 1
        )
        mat[:, mine] = jnp.zeros((n, 128), F32)
        mat[...] = mat[...] - dot3(rows, panel, TN)
        mat[mine, :] = panel
        if k in dict(outer):
            dict(outer)[k]()


def row_dot(vec, parts):
    a, b, c = [part.astype(F32) for part in split3(vec)]
    index = lax.broadcasted_iota(jnp.int32, (16, vec.shape[1]), 0)
    left = jnp.where(index == 0, a, jnp.where(index == 1, b, jnp.where(index == 2, c, 0.0))).astype(BF)
    out = dot(left, parts[0], NN) + dot(left, parts[1], NN)
    return jnp.sum(out, axis=0, keepdims=True)


SLAB = 16
TILES = R // 128
SYM = 5 * SLAB
PIECE = SYM + 8
CUT = 48
HALF = 8
SIDE = 4


def piece_tiles(group):
    low = group + 1
    return [(False, t) for t in range(low)] + [(True, t) for t in range(5 - low)]


def slab_rows(index):
    return pl.ds(pl.multiple_of(index * SLAB, SLAB), SLAB)


def pack(full, vec, pieces):
    pieces[:, :, SYM:PIECE, :] = jnp.zeros((SIDE, SIDE, 8, 128), F32)
    for group in range(2):

        def body(i, carry):
            s = group * HALF + i
            for t, (high, tile) in enumerate(piece_tiles(group)):
                rows = slab_rows(2 * SIDE * SIDE - 1 - s if high else s)
                pieces[lax.div(s, SIDE), lax.rem(s, SIDE), SLAB * t : SLAB * t + SLAB, :] = full[
                    rows, 128 * tile : 128 * tile + 128
                ]
            return carry

        lax.fori_loop(0, HALF, body, 0)
    for c in range(TILES):
        pieces[c, 0, SYM:PIECE, :] = vec[0:8, 128 * c : 128 * c + 128]


def unpack(pieces, full, vec):
    for group in range(2):

        def body(i, carry):
            s = group * HALF + i
            for t, (high, tile) in enumerate(piece_tiles(group)):
                rows = slab_rows(2 * SIDE * SIDE - 1 - s if high else s)
                full[rows, 128 * tile : 128 * tile + 128] = pieces[
                    lax.div(s, SIDE), lax.rem(s, SIDE), SLAB * t : SLAB * t + SLAB, :
                ]
            return carry

        lax.fori_loop(0, HALF, body, 0)
    for i in range(TILES):
        for j in range(i):
            full[128 * j : 128 * j + 128, 128 * i : 128 * i + 128] = full[
                128 * i : 128 * i + 128, 128 * j : 128 * j + 128
            ].T
    for c in range(TILES):
        vec[0:8, 128 * c : 128 * c + 128] = pieces[c, 0, SYM:PIECE, :]


class Exchange:
    def __init__(self, axis, source, into, send_sem, recv_sem):
        self.axis, self.source, self.into, self.send_sem, self.recv_sem = axis, source, into, send_sem, recv_sem
        self.n = lax.axis_size(axis)
        self.me = lax.axis_index(axis)

    def copy(self, d):
        peer = lax.rem(self.me + d, self.n)
        return pltpu.make_async_remote_copy(
            src_ref=self.source(peer),
            dst_ref=self.into(d),
            send_sem=self.send_sem.at[d],
            recv_sem=self.recv_sem.at[d],
            device_id={self.axis: peer},
            device_id_type=MESH,
        )

    def each(self, act):
        def body(d, carry):
            act(self.copy(d))
            return carry

        lax.fori_loop(1, self.n, body, 0)

    def start(self):
        self.each(lambda copy: copy.start())

    def wait_recv(self):
        self.each(lambda copy: copy.wait_recv())

    def wait_send(self):
        self.each(lambda copy: copy.wait_send())


class Grid:
    def __init__(self, source, cut, from_x, from_y, mid_x, mid_y, late_x, late_y, result, send_sem, recv_sem):
        self.source, self.cut, self.result = source, cut, result
        self.from_x, self.from_y, self.mid_x, self.mid_y = from_x, from_y, mid_x, mid_y
        self.late_x, self.late_y = late_x, late_y
        self.send_sem, self.recv_sem = send_sem, recv_sem
        sub = lax.axis_index("sub")
        self.px, self.py = lax.div(sub, SIDE), lax.rem(sub, SIDE)
        self.first, self.rest = slice(0, cut), slice(cut, source.shape[2])

    def copies(self, phase):
        out = []
        px, py, first, rest = self.px, self.py, self.first, self.rest
        source, result = self.source, self.result
        for d in range(1, SIDE):
            x, y = lax.rem(px + d, SIDE), lax.rem(py + d, SIDE)
            at_x, at_y = x * SIDE + py, px * SIDE + y
            if phase == 0:
                pair = (
                    (source.at[x, :, first, :], self.from_x.at[d], at_x),
                    (source.at[:, y, rest, :], self.from_y.at[d], at_y),
                )
            elif phase == 1:
                pair = (
                    (self.mid_x.at[y], self.late_x.at[d], at_y),
                    (self.mid_y.at[x], self.late_y.at[d], at_x),
                )
            elif phase == 2:
                one, two = result.at[px, py, first, :], result.at[px, py, rest, :]
                pair = ((one, one, at_y), (two, two, at_x))
            else:
                one, two = result.at[px, :, first, :], result.at[:, py, rest, :]
                pair = ((one, one, at_x), (two, two, at_y))
            for k, (src, dst, peer) in enumerate(pair):
                out.append(
                    pltpu.make_async_remote_copy(
                        src_ref=src,
                        dst_ref=dst,
                        send_sem=self.send_sem.at[phase, k, d],
                        recv_sem=self.recv_sem.at[phase, k, d],
                        device_id={"sub": peer},
                        device_id_type=MESH,
                    )
                )
        return out

    def start(self, phase):
        for copy in self.copies(phase):
            copy.start()

    def wait_recv(self, phase):
        for copy in self.copies(phase):
            copy.wait_recv()

    def wait_send(self, phases):
        for phase in phases:
            for copy in self.copies(phase):
                copy.wait_send()

    def middle(self):
        self.mid_x[...] = self.source[self.px, :, self.first, :] + jnp.sum(self.from_x[1:], axis=0)
        self.mid_y[...] = self.source[:, self.py, self.rest, :] + jnp.sum(self.from_y[1:], axis=0)

    def finish(self, target):
        target[self.first, :] = self.mid_x[self.py] + jnp.sum(self.late_x[1:], axis=0)
        target[self.rest, :] = self.mid_y[self.px] + jnp.sum(self.late_y[1:], axis=0)


def first_row(vec, rows):
    total = jnp.sum(vec, axis=0, keepdims=True)
    index = lax.broadcasted_iota(jnp.int32, (rows, vec.shape[1]), 0)
    return jnp.where(index == 0, total, 0.0)


def kernel(
    count, tau, obs, basis_hbm, fine_hbm, group_hbm, root_hbm,
    root_out, group_out, fine_out, field_out,
    basis, mat, block, prior1, prior0, cross, high, low, xvec, s11, s01, s00, vec1, vec0, inv1, a01, a1, b0,
    mid0, recvg, all0, bufs1, bufs01, bufs0, load_sem, sem_s, sem_r, sema_s, sema_r, semg_s, semg_r,
):
    sub = lax.axis_index("sub")
    grp = lax.axis_index("grp")
    nsub, ngrp = lax.axis_size("sub"), lax.axis_size("grp")
    rows = R // nsub

    def load(k):
        pairs = (
            (basis_hbm.at[2], basis.at[2]), (fine_hbm.at[0], mat), (basis_hbm.at[1], basis.at[1]),
            (basis_hbm.at[0], basis.at[0]), (group_hbm.at[0], prior1), (root_hbm, prior0),
        )
        return pltpu.make_async_copy(pairs[k][0], pairs[k][1], load_sem.at[k])

    for k in range(6):
        load(k).start()
    barrier = pltpu.get_barrier_semaphore()

    def greet(axis, me, n):
        def body(d, carry):
            pl.semaphore_signal(
                barrier, inc=1, device_id={axis: lax.rem(me + d, n)}, device_id_type=MESH
            )
            return carry

        lax.fori_loop(1, n, body, 0)

    greet("sub", sub, nsub)
    greet("grp", grp, ngrp)

    px, py = lax.div(sub, SIDE), lax.rem(sub, SIDE)
    send1, all1 = bufs1[0], bufs1[7]
    grid1 = Grid(send1, CUT, *bufs1[1:], sem_s.at[0], sem_r.at[0])
    grid01 = Grid(s01, rows // 2, *bufs01, a01, sem_s.at[1], sem_r.at[1])
    send0 = bufs0[0]
    grid0 = Grid(send0, CUT, *bufs0[1:], None, sem_s.at[2], sem_r.at[2])
    gather0 = Exchange("sub", lambda peer: all0.at[px, py], lambda d: all0.at[px, py], sema_s, sema_r)
    across = Exchange("grp", lambda peer: mid0, lambda d: recvg.at[d], semg_s, semg_r)

    slots = basis.shape[1]
    t = tau[0]
    n = count[0]
    valid = lax.broadcasted_iota(jnp.int32, (slots, 1), 0) < n
    chunks = slots // 128
    index = lax.broadcasted_iota(jnp.int32, (chunks, 128), 0)
    slot = index * 128 + lax.broadcasted_iota(jnp.int32, (chunks, 128), 1)
    y = jnp.where(slot < n, obs[...].astype(F32), 0.0)
    y = jnp.concatenate([jnp.where(index == c, y, 0.0) for c in range(chunks)], 1).astype(BF)

    def masked(a):
        block = basis[a]
        return jnp.where(valid, block, jnp.zeros_like(block))

    load(0).wait()
    m2 = masked(2)
    load(1).wait()
    mat[...] = mat[...] + t * dot(basis[2], m2, TN)
    cross[2 * R : 2 * R + 16, :] = first_row(t * dot(y, basis[2], NN), 16)
    load(2).wait()
    cross[0:R, :] = t * dot(basis[1], m2, TN)
    m1 = masked(1)
    s11[...] = t * dot(basis[1], m1, TN)
    vec1[...] = first_row(t * dot(y, basis[1], NN), 16)
    negative_inverse(mat, block)

    inv = split2(mat[...])
    c1 = split2(cross[0:R, :])
    x1 = split2(dot3(c1, inv, NN))
    high[0:R, :], low[0:R, :] = x1
    xy = dot3(cross[2 * R : 2 * R + 16, :], inv, NN)
    xvec[...] = xy
    s11[...] = s11[...] + dot3(x1, c1, NT)
    vec1[...] = vec1[...] + dot3(xy, c1, NT)
    pack(s11, vec1, send1)
    pl.semaphore_wait(barrier, nsub + ngrp - 2)
    grid1.start(0)

    load(3).wait()
    m0 = masked(0)
    cross[R : 2 * R, :] = t * dot(m0, basis[2], TN)
    c0 = split2(cross[R : 2 * R, :])
    x0 = split2(dot3(c0, inv, NN))
    high[R : 2 * R, :], low[R : 2 * R, :] = x0
    s01[...] = (t * dot(m0, basis[1], TN) + dot3(x0, c1, NT)).reshape(SIDE, SIDE, rows, R)
    grid01.start(0)
    grid1.wait_recv(0)
    grid1.middle()
    grid1.start(1)
    s00[...] = t * dot(m0, basis[0], TN) + dot3(x0, c0, NT)
    vec0[...] = first_row(t * dot(y, basis[0], NN), 16) + dot3(xy, c0, NT)
    pack(s00, vec0, send0)
    grid1.wait_recv(1)
    grid1.finish(all1.at[px, py])
    grid1.start(2)
    grid01.wait_recv(0)
    grid01.middle()
    grid01.start(1)
    grid1.wait_recv(2)
    grid1.start(3)
    grid01.wait_recv(1)
    grid01.finish(a01.at[px, py])
    grid01.start(2)
    grid1.wait_recv(3)
    unpack(all1, inv1, a1)
    load(4).wait()
    inv1[...] = inv1[...] + prior1[...]
    def one():
        grid01.wait_recv(2)
        grid01.start(3)

    def three():
        grid0.wait_recv(0)
        grid0.middle()
        grid0.start(1)

    negative_inverse(inv1, block, inner=((0, one), (2, three)), outer=((0, lambda: grid0.start(0)),))
    grid0.wait_recv(1)
    grid0.finish(mid0)
    grid01.wait_recv(3)

    inv = split2(inv1[...])
    both = split2(a01[...].reshape(R, R))
    mine, mirror = lax.div(sub, 2), lax.div(2 * nsub - 1 - sub, 2)
    half = pl.multiple_of(lax.rem(sub, 2) * SLAB, SLAB)
    left = jnp.concatenate(
        [
            a01[lax.div(mine, SIDE), lax.rem(mine, SIDE), pl.ds(half, SLAB), :],
            a01[lax.div(mirror, SIDE), lax.rem(mirror, SIDE), pl.ds(pl.multiple_of(SLAB - half, SLAB), SLAB), :],
            a1[...], jnp.zeros((8, R), F32),
        ],
        0,
    )
    left = dot3(left, inv, NN)
    term = dot3(left, both, NT)
    upper = sub >= HALF
    for k, (one, two) in enumerate(zip(piece_tiles(0), piece_tiles(1))):
        parts = [
            term[SLAB * hi : SLAB * hi + SLAB, 128 * tile : 128 * tile + 128] for hi, tile in (one, two)
        ]
        place = slice(SLAB * k, SLAB * k + SLAB)
        mid0[place, :] = mid0[place, :] + jnp.where(upper, parts[1], parts[0])
    extra = jnp.zeros((8, 128), F32)
    for c in range(TILES):
        extra = extra + jnp.where(sub == 4 * c, term[2 * SLAB : 2 * SLAB + 8, 128 * c : 128 * c + 128], 0.0)
    mid0[SYM:PIECE, :] = mid0[SYM:PIECE, :] + extra
    across.start()
    lead1 = split2(dot3(both, inv, NN))
    last1 = left[2 * SLAB : 2 * SLAB + 1, :]
    fine1 = (high[0:R, :], low[0:R, :])
    across.wait_recv()
    recvg[0] = mid0[...]
    total = recvg[grp]
    for g in range(1, ngrp):
        total = total + recvg[lax.rem(grp - g + ngrp, ngrp)]
    all0[px, py] = total
    gather0.start()
    lead2 = split2(high[R : 2 * R, :].astype(F32) + low[R : 2 * R, :].astype(F32) + dot3(lead1, fine1, NN))
    last2 = xvec[0:1, :] + row_dot(last1, fine1)
    gather0.wait_recv()
    unpack(all0, mat, b0)
    load(5).wait()
    mat[...] = mat[...] + prior0[...]
    negative_inverse(mat, block)
    mean0 = -row_dot(b0[0:1, :], split2(mat[...]))
    mean1 = row_dot(mean0, lead1) - last1
    mean2 = row_dot(mean0, lead2) - last2
    root_out[...] = mean0
    group_out[...] = mean1
    fine_out[...] = mean2

    def fit(mean, a):
        left = jnp.broadcast_to(mean, (16, R)).astype(BF)
        return dot(left, basis[a], NT)

    field_out[...] = (fit(mean0, 0) + fit(mean1, 1) + fit(mean2, 2))[0:1, :]
    grid1.wait_send(range(4))
    grid01.wait_send(range(4))
    grid0.wait_send(range(2))
    across.wait_send()
    gather0.wait_send()


def place_kernel(root, group, fine, field, root_out, group_out, fine_out, field_out):
    lanes = root_out.shape[1]
    first = lax.axis_index("sub") * lanes
    tile = pl.multiple_of(lax.div(first, 128) * 128, 128)
    shift = lax.rem(128 - (first - tile), 128)
    for whole, out in ((root, root_out), (group, group_out)):
        out[...] = pltpu.roll(jnp.broadcast_to(whole[:, pl.ds(tile, 128)], (8, 128)), shift, 1)[0:1, 0:lanes]
    fine_out[...] = fine[...]
    field_out[...] = field[...]


def shape(*dims):
    return jax.ShapeDtypeStruct(dims, F32)


def shards(basis, observations, counts, noise_prec, prior_fine, prior_group, prior_root):
    slots = basis.shape[1]
    nsub, ngrp = lax.axis_size("sub"), lax.axis_size("grp")

    def buf(*dims, kind=F32):
        return pltpu.VMEM(dims, kind)

    def halves(one, two, lanes):
        sizes = (one, two)
        return (
            [buf(SIDE, SIDE, size, lanes) for size in sizes] + [buf(SIDE, size, lanes) for size in sizes]
            + [buf(SIDE, size, lanes) for size in sizes]
        )

    root, group, fine, field = pl.pallas_call(
        kernel,
        name="levels",
        out_shape=[shape(1, R), shape(1, R), shape(1, R), shape(1, slots)],
        in_specs=[SM, SM, VM, HB, HB, HB, HB],
        out_specs=[VM] * 4,
        scratch_shapes=[
            buf(3, slots, R, kind=BF), buf(R, R), buf(128, 128), buf(R, R), buf(R, R), buf(2 * R + 16, R),
            buf(2 * R, R, kind=BF), buf(2 * R, R, kind=BF), buf(16, R),
            buf(R, R), buf(SIDE, SIDE, R // nsub, R), buf(R, R), buf(16, R), buf(16, R),
            buf(R, R), buf(SIDE, SIDE, R // nsub, R), buf(8, R), buf(8, R),
            buf(PIECE, 128), buf(ngrp, PIECE, 128), buf(SIDE, SIDE, PIECE, 128),
            [buf(SIDE, SIDE, PIECE, 128), *halves(CUT, PIECE - CUT, 128), buf(SIDE, SIDE, PIECE, 128)],
            halves(R // nsub // 2, R // nsub // 2, R),
            [buf(SIDE, SIDE, PIECE, 128), *halves(CUT, PIECE - CUT, 128)],
            pltpu.SemaphoreType.DMA((6,)),
            pltpu.SemaphoreType.DMA((3, 4, 2, SIDE)), pltpu.SemaphoreType.DMA((3, 4, 2, SIDE)),
            pltpu.SemaphoreType.DMA((nsub,)), pltpu.SemaphoreType.DMA((nsub,)),
            pltpu.SemaphoreType.DMA((ngrp,)), pltpu.SemaphoreType.DMA((ngrp,)),
        ],
        compiler_params=pltpu.CompilerParams(collective_id=0, has_side_effects=True, vmem_limit_bytes=60 << 20),
    )(counts, noise_prec, observations.reshape(slots // 128, 128), basis, prior_fine, prior_group, prior_root)
    outs = pl.pallas_call(
        place_kernel,
        name="place",
        out_shape=[shape(1, R // nsub), shape(1, R // nsub), shape(1, R), shape(1, slots)],
        in_specs=[VM] * 4,
        out_specs=[VM] * 4,
    )(root, group, fine, field)
    return tuple(out[0] for out in outs)


def solution(mesh):
    in_specs = (
        P(None, ("grp", "sub"), None),
        P(("grp", "sub")),
        P(("grp", "sub")),
        P(("grp", "sub")),
        P(("grp", "sub"), None, None),
        P("grp", None, None),
        P(),
    )
    out_specs = (P("sub"), P(("grp", "sub")), P(("grp", "sub")), P(("grp", "sub")))
    return jax.shard_map(shards, mesh=mesh, in_specs=in_specs, out_specs=out_specs, check_vma=False)
```

```python
import functools

import jax
import jax.numpy as jnp
from jax import lax
from jax.experimental import pallas as pl
from jax.experimental.pallas import tpu as pltpu
from jax.sharding import PartitionSpec as P

F32 = jnp.float32
BF = jnp.bfloat16
MESH = pl.DeviceIdType.MESH
R = 512
NB = 16
AUG = R + 16
VM = pl.BlockSpec(memory_space=pltpu.VMEM)
SM = pl.BlockSpec(memory_space=pltpu.SMEM)
HB = pl.BlockSpec(memory_space=pl.ANY)
NN = (((1,), (0,)), ((), ()))
TN = (((0,), (0,)), ((), ()))
NT = (((1,), (1,)), ((), ()))


def split2(x):
    high = x.astype(BF)
    return high, (x - high.astype(F32)).astype(BF)


def split3(x):
    high = x.astype(BF)
    rest = x - high.astype(F32)
    mid = rest.astype(BF)
    return high, mid, (rest - mid.astype(F32)).astype(BF)


def dot(left, right, dims):
    return lax.dot_general(left, right, dims, preferred_element_type=F32)


def dot3(left, right, dims):
    a, b = left if isinstance(left, tuple) else split2(left)
    c, d = right if isinstance(right, tuple) else split2(right)
    (k,), (m,) = dims[0]
    return dot(jnp.concatenate([a, a, b], k), jnp.concatenate([c, d, c], m), dims)


def splat_columns(rows, first, lane):
    return [
        jnp.broadcast_to(jnp.sum(jnp.where(lane == first + j, rows, 0.0), axis=1, keepdims=True), (NB, 128))
        for j in range(NB)
    ]


def eliminate(rows, first, sub, lane):
    inside = (lane >= first) & (lane < first + NB)
    eye = jnp.where(lane == first + sub, -1.0, 0.0)
    work = jnp.stack(splat_columns(rows, first, lane) + [jnp.where(inside, eye, rows)], 0)
    for i in range(NB):
        mine = sub[0:8] == i % 8
        inv = 1.0 / jnp.broadcast_to(work[0, i : i + 1, :], (8, 128))
        rest = work[1:]
        pivot_row = jnp.broadcast_to(rest[:, i : i + 1, :], (rest.shape[0], 8, 128))
        out = []
        for g in range(NB // 8):
            place = slice(8 * g, 8 * g + 8)
            base, mult = rest[:, place], -work[0, place] * inv
            if g == i // 8:
                base, mult = jnp.where(mine[None], 0.0, base), jnp.where(mine, inv, mult)
            out.append(base + mult[None] * pivot_row)
        work = jnp.concatenate(out, 1)
    return work[0]


def sweep_block(mat):
    count = 128 // NB
    sub = lax.broadcasted_iota(jnp.int32, (NB, 128), 0)
    lane = lax.broadcasted_iota(jnp.int32, (NB, 128), 1)

    def inside(p):
        return (lane >= p * NB) & (lane < p * NB + NB)

    def place(p):
        return pl.ds(pl.multiple_of(p * NB, NB), NB)

    def update(p, rows, panel):
        mat[...] = jnp.where(inside(p)[0:1], 0.0, mat[...]) - dot3(rows, panel, TN)
        mat[place(p), :] = panel

    def advance(following, p, panel):
        cols = splat_columns(following, p * NB, lane)
        terms = [cols[m] * jnp.broadcast_to(panel[m : m + 1, :], (NB, 128)) for m in range(NB)]
        while len(terms) > 1:
            terms = [terms[i] + terms[i + 1] for i in range(0, len(terms), 2)]
        return jnp.where(inside(p), 0.0, following) - terms[0]

    def body(p, carry):
        rows, before, panel_before = carry
        update(p - 1, before, panel_before)
        following = mat[place(jnp.minimum(p + 1, count - 1)), :]
        panel = eliminate(rows, p * NB, sub, lane)
        return advance(following, p, panel), rows, panel

    rows = mat[0:NB, :]
    panel = eliminate(rows, 0, sub, lane)
    start = (advance(mat[NB : 2 * NB, :], 0, panel), rows, panel)
    _, rows, panel = lax.fori_loop(1, count, body, start)
    update(count - 1, rows, panel)


def negative_inverse(mat, block, ready=None, inner=(), outer=()):
    n = mat.shape[0]
    for k in range(n // 128):
        mine = slice(128 * k, 128 * k + 128)
        if k > 0 or ready is None:
            block[...] = mat[mine, mine]
        sweep_block(block)
        if k in dict(inner):
            dict(inner)[k]()
        if k == 0 and ready is not None:
            ready()
        own = block[...]
        rows = split2(mat[mine, :])
        panel = -dot3(own, rows, NN)
        panel = jnp.concatenate(
            [own if c == k else panel[:, 128 * c : 128 * c + 128] for c in range(n // 128)], 1
        )
        mat[:, mine] = jnp.zeros((n, 128), F32)
        mat[...] = mat[...] - dot3(rows, panel, TN)
        mat[mine, :] = panel
        if k in dict(outer):
            dict(outer)[k]()


def row_dot(vec, parts):
    a, b, c = [part.astype(F32) for part in split3(vec)]
    index = lax.broadcasted_iota(jnp.int32, (16, vec.shape[1]), 0)
    left = jnp.where(index == 0, a, jnp.where(index == 1, b, jnp.where(index == 2, c, 0.0))).astype(BF)
    out = dot(left, parts[0], NN) + dot(left, parts[1], NN)
    return jnp.sum(out, axis=0, keepdims=True)


SLAB = 16
TILES = R // 128
SYM = 5 * SLAB
PIECE = SYM + 8
CUT = 48
HALF = 8
SIDE = 4


def piece_tiles(group):
    low = group + 1
    return [(False, t) for t in range(low)] + [(True, t) for t in range(5 - low)]


def slab_rows(index):
    return pl.ds(pl.multiple_of(index * SLAB, SLAB), SLAB)


def pack(full, vec, pieces):
    pieces[:, :, SYM:PIECE, :] = jnp.zeros((SIDE, SIDE, 8, 128), F32)
    for group in range(2):

        def body(i, carry):
            s = group * HALF + i
            for t, (high, tile) in enumerate(piece_tiles(group)):
                rows = slab_rows(2 * SIDE * SIDE - 1 - s if high else s)
                pieces[lax.div(s, SIDE), lax.rem(s, SIDE), SLAB * t : SLAB * t + SLAB, :] = full[
                    rows, 128 * tile : 128 * tile + 128
                ]
            return carry

        lax.fori_loop(0, HALF, body, 0)
    for c in range(TILES):
        pieces[c, 0, SYM:PIECE, :] = vec[0:8, 128 * c : 128 * c + 128]


def unpack(pieces, full, vec):
    for group in range(2):

        def body(i, carry):
            s = group * HALF + i
            for t, (high, tile) in enumerate(piece_tiles(group)):
                rows = slab_rows(2 * SIDE * SIDE - 1 - s if high else s)
                full[rows, 128 * tile : 128 * tile + 128] = pieces[
                    lax.div(s, SIDE), lax.rem(s, SIDE), SLAB * t : SLAB * t + SLAB, :
                ]
            return carry

        lax.fori_loop(0, HALF, body, 0)
    for i in range(TILES):
        for j in range(i):
            full[128 * j : 128 * j + 128, 128 * i : 128 * i + 128] = full[
                128 * i : 128 * i + 128, 128 * j : 128 * j + 128
            ].T
    for c in range(TILES):
        vec[0:8, 128 * c : 128 * c + 128] = pieces[c, 0, SYM:PIECE, :]


def first_block(pieces, prior, block):
    for s in range(HALF):
        rows = slice(SLAB * s, SLAB * s + SLAB)
        block[rows, :] = pieces[s // SIDE, s % SIDE, 0:SLAB, :] + prior[rows, 0:128]


class Exchange:
    def __init__(self, axis, source, into, send_sem, recv_sem):
        self.axis, self.source, self.into, self.send_sem, self.recv_sem = axis, source, into, send_sem, recv_sem
        self.n = lax.axis_size(axis)
        self.me = lax.axis_index(axis)

    def copy(self, d):
        peer = lax.rem(self.me + d, self.n)
        return pltpu.make_async_remote_copy(
            src_ref=self.source(peer),
            dst_ref=self.into(d),
            send_sem=self.send_sem.at[d],
            recv_sem=self.recv_sem.at[d],
            device_id={self.axis: peer},
            device_id_type=MESH,
        )

    def each(self, act):
        def body(d, carry):
            act(self.copy(d))
            return carry

        lax.fori_loop(1, self.n, body, 0)

    def start(self):
        self.each(lambda copy: copy.start())

    def wait_recv(self):
        self.each(lambda copy: copy.wait_recv())

    def wait_send(self):
        self.each(lambda copy: copy.wait_send())


class Grid:
    def __init__(self, source, cut, from_x, from_y, mid_x, mid_y, late_x, late_y, result, send_sem, recv_sem, early=0):
        self.source, self.cut, self.result = source, cut, result
        self.from_x, self.from_y, self.mid_x, self.mid_y = from_x, from_y, mid_x, mid_y
        self.late_x, self.late_y = late_x, late_y
        self.send_sem, self.recv_sem = send_sem, recv_sem
        sub = lax.axis_index("sub")
        self.px, self.py = lax.div(sub, SIDE), lax.rem(sub, SIDE)
        self.first, self.rest = slice(0, cut), slice(cut, source.shape[2])
        self.early = early

    def copies(self, phase):
        out = []
        px, py, first, rest = self.px, self.py, self.first, self.rest
        source, result = self.source, self.result
        for d in range(1, SIDE):
            x, y = lax.rem(px + d, SIDE), lax.rem(py + d, SIDE)
            at_x, at_y = x * SIDE + py, px * SIDE + y
            if phase == 0:
                pair = (
                    (source.at[x, :, first, :], self.from_x.at[d], at_x),
                    (source.at[:, y, rest, :], self.from_y.at[d], at_y),
                )
            elif phase == 1:
                pair = (
                    (self.mid_x.at[y], self.late_x.at[d], at_y),
                    (self.mid_y.at[x], self.late_y.at[d], at_x),
                )
            elif phase == 2:
                one, two = result.at[px, py, first, :], result.at[px, py, rest, :]
                pair = ((one, one, at_y), (two, two, at_x))
            elif phase == 3:
                one, two = result.at[px, :, self.early : self.cut, :], result.at[:, py, rest, :]
                pair = ((one, one, at_x), (two, two, at_y))
            else:
                one = result.at[px, :, 0 : self.early, :]
                pair = ((one, one, at_x),)
            for k, (src, dst, peer) in enumerate(pair):
                out.append(
                    pltpu.make_async_remote_copy(
                        src_ref=src,
                        dst_ref=dst,
                        send_sem=self.send_sem.at[phase, k, d],
                        recv_sem=self.recv_sem.at[phase, k, d],
                        device_id={"sub": peer},
                        device_id_type=MESH,
                    )
                )
        return out

    def start(self, phase):
        for copy in self.copies(phase):
            copy.start()

    def wait_recv(self, phase):
        for copy in self.copies(phase):
            copy.wait_recv()

    def wait_send(self, phases):
        for phase in phases:
            for copy in self.copies(phase):
                copy.wait_send()

    def middle(self):
        self.mid_x[...] = self.source[self.px, :, self.first, :] + jnp.sum(self.from_x[1:], axis=0)
        self.mid_y[...] = self.source[:, self.py, self.rest, :] + jnp.sum(self.from_y[1:], axis=0)

    def finish(self, target):
        target[self.first, :] = self.mid_x[self.py] + jnp.sum(self.late_x[1:], axis=0)
        target[self.rest, :] = self.mid_y[self.px] + jnp.sum(self.late_y[1:], axis=0)


def first_row(vec, rows):
    total = jnp.sum(vec, axis=0, keepdims=True)
    index = lax.broadcasted_iota(jnp.int32, (rows, vec.shape[1]), 0)
    return jnp.where(index == 0, total, 0.0)


def kernel(
    count, tau, obs, basis_hbm, fine_hbm, group_hbm, root_hbm,
    root_out, group_out, fine_out, field_out,
    basis, mat, block, prior1, prior0, cross, high, low, xvec, s11, s01, s00, vec1, vec0, inv1, a01, a1, b0,
    mid0, recvg, all0, bufs1, bufs01, bufs0, load_sem, sem_s, sem_r, sema_s, sema_r, semg_s, semg_r,
):
    sub = lax.axis_index("sub")
    grp = lax.axis_index("grp")
    nsub, ngrp = lax.axis_size("sub"), lax.axis_size("grp")
    rows = R // nsub

    def load(k):
        pairs = (
            (basis_hbm.at[2], basis.at[2]), (fine_hbm.at[0], mat), (basis_hbm.at[1], basis.at[1]),
            (basis_hbm.at[0], basis.at[0]), (group_hbm.at[0], prior1), (root_hbm, prior0),
        )
        return pltpu.make_async_copy(pairs[k][0], pairs[k][1], load_sem.at[k])

    for k in range(6):
        load(k).start()
    barrier = pltpu.get_barrier_semaphore()

    def greet(axis, me, n):
        def body(d, carry):
            pl.semaphore_signal(
                barrier, inc=1, device_id={axis: lax.rem(me + d, n)}, device_id_type=MESH
            )
            return carry

        lax.fori_loop(1, n, body, 0)

    greet("sub", sub, nsub)
    greet("grp", grp, ngrp)

    px, py = lax.div(sub, SIDE), lax.rem(sub, SIDE)
    send1, all1 = bufs1[0], bufs1[7]
    grid1 = Grid(send1, CUT, *bufs1[1:], sem_s.at[0], sem_r.at[0], early=SLAB)
    grid01 = Grid(s01, rows // 2, *bufs01, a01, sem_s.at[1], sem_r.at[1])
    send0 = bufs0[0]
    grid0 = Grid(send0, CUT, *bufs0[1:], None, sem_s.at[2], sem_r.at[2])
    tile0, tiles0 = all0.at[px, py, 0:SLAB, :], all0.at[px, py, SLAB:PIECE, :]
    early0 = Exchange("sub", lambda peer: tile0, lambda d: tile0, sema_s.at[0], sema_r.at[0])
    gather0 = Exchange("sub", lambda peer: tiles0, lambda d: tiles0, sema_s.at[1], sema_r.at[1])
    across = Exchange("grp", lambda peer: mid0, lambda d: recvg.at[d], semg_s, semg_r)

    slots = basis.shape[1]
    t = tau[0]
    n = count[0]
    valid = lax.broadcasted_iota(jnp.int32, (slots, 1), 0) < n
    chunks = slots // 128
    index = lax.broadcasted_iota(jnp.int32, (chunks, 128), 0)
    slot = index * 128 + lax.broadcasted_iota(jnp.int32, (chunks, 128), 1)
    y = jnp.where(slot < n, obs[...].astype(F32), 0.0)
    y = jnp.concatenate([jnp.where(index == c, y, 0.0) for c in range(chunks)], 1).astype(BF)

    def masked(a):
        block = basis[a]
        return jnp.where(valid, block, jnp.zeros_like(block))

    load(0).wait()
    m2 = masked(2)
    load(1).wait()
    mat[...] = mat[...] + t * dot(basis[2], m2, TN)
    cross[R:AUG, :] = first_row(t * dot(y, basis[2], NN), 16)
    load(2).wait()
    cross[0:R, :] = t * dot(basis[1], m2, TN)
    m1 = masked(1)
    s11[...] = t * dot(basis[1], m1, TN)
    vec1[...] = first_row(t * dot(y, basis[1], NN), 16)
    negative_inverse(mat, block)

    inv = split2(mat[...])
    cy = split2(cross[0:AUG, :])
    c1 = tuple(part[0:R] for part in cy)
    x1 = dot3(cy, inv, NN)
    xvec[...] = x1[R:AUG]
    x1 = split2(x1)
    high[0:R, :], low[0:R, :] = x1[0][0:R], x1[1][0:R]
    xy = tuple(part[R:AUG] for part in x1)
    add = dot3(x1, c1, NT)
    s11[...] = s11[...] + add[0:R]
    vec1[...] = vec1[...] + add[R:AUG]
    pack(s11, vec1, send1)
    pl.semaphore_wait(barrier, nsub + ngrp - 2)
    grid1.start(0)

    load(3).wait()
    m0 = masked(0)
    c0 = split2(t * dot(m0, basis[2], TN))
    x0 = split2(dot3(c0, inv, NN))
    high[R : 2 * R, :], low[R : 2 * R, :] = x0
    s01[...] = (t * dot(m0, basis[1], TN) + dot3(x0, c1, NT)).reshape(SIDE, SIDE, rows, R)
    grid01.start(0)
    grid1.wait_recv(0)
    grid1.middle()
    grid1.start(1)
    s00[...] = t * dot(m0, basis[0], TN) + dot3(x0, c0, NT)
    vec0[...] = first_row(t * dot(y, basis[0], NN), 16) + dot3(xy, c0, NT)
    pack(s00, vec0, send0)
    grid1.wait_recv(1)
    grid1.finish(all1.at[px, py])
    grid1.start(2)
    grid01.wait_recv(0)
    grid01.middle()
    grid01.start(1)
    grid1.wait_recv(2)
    grid1.start(4)
    grid1.start(3)
    grid01.wait_recv(1)
    grid01.finish(a01.at[px, py])
    grid01.start(2)
    load(4).wait()
    grid1.wait_recv(4)
    first_block(all1, prior1, block)

    def ready1():
        grid1.wait_recv(3)
        unpack(all1, inv1, a1)
        inv1[...] = inv1[...] + prior1[...]

    def one():
        grid01.wait_recv(2)
        grid01.start(3)

    def three():
        grid0.wait_recv(0)
        grid0.middle()
        grid0.start(1)

    negative_inverse(inv1, block, ready1, inner=((0, one), (2, three)), outer=((0, lambda: grid0.start(0)),))
    grid0.wait_recv(1)
    grid0.finish(mid0)
    grid01.wait_recv(3)

    inv = split2(inv1[...])
    both = split2(a01[...].reshape(R, R))
    mine, mirror = lax.div(sub, 2), lax.div(2 * nsub - 1 - sub, 2)
    half = pl.multiple_of(lax.rem(sub, 2) * SLAB, SLAB)
    left = jnp.concatenate(
        [
            a01[lax.div(mine, SIDE), lax.rem(mine, SIDE), pl.ds(half, SLAB), :],
            a01[lax.div(mirror, SIDE), lax.rem(mirror, SIDE), pl.ds(pl.multiple_of(SLAB - half, SLAB), SLAB), :],
            a1[...], jnp.zeros((8, R), F32),
        ],
        0,
    )
    left = dot3(left, inv, NN)
    term = dot3(left, both, NT)
    upper = sub >= HALF
    for k, (one, two) in enumerate(zip(piece_tiles(0), piece_tiles(1))):
        parts = [
            term[SLAB * hi : SLAB * hi + SLAB, 128 * tile : 128 * tile + 128] for hi, tile in (one, two)
        ]
        place = slice(SLAB * k, SLAB * k + SLAB)
        mid0[place, :] = mid0[place, :] + jnp.where(upper, parts[1], parts[0])
    extra = jnp.zeros((8, 128), F32)
    for c in range(TILES):
        extra = extra + jnp.where(sub == 4 * c, term[2 * SLAB : 2 * SLAB + 8, 128 * c : 128 * c + 128], 0.0)
    mid0[SYM:PIECE, :] = mid0[SYM:PIECE, :] + extra
    across.start()
    lead1 = split2(dot3(both, inv, NN))
    last1 = left[2 * SLAB : 2 * SLAB + 1, :]
    fine1 = (high[0:R, :], low[0:R, :])
    across.wait_recv()
    recvg[0] = mid0[...]
    total = recvg[grp]
    for g in range(1, ngrp):
        total = total + recvg[lax.rem(grp - g + ngrp, ngrp)]
    all0[px, py] = total
    early0.start()
    gather0.start()
    lead2 = split2(high[R : 2 * R, :].astype(F32) + low[R : 2 * R, :].astype(F32) + dot3(lead1, fine1, NN))
    last2 = xvec[0:1, :] + row_dot(last1, fine1)
    load(5).wait()
    early0.wait_recv()
    first_block(all0, prior0, block)

    def ready0():
        gather0.wait_recv()
        unpack(all0, mat, b0)
        mat[...] = mat[...] + prior0[...]

    negative_inverse(mat, block, ready0)
    mean0 = -row_dot(b0[0:1, :], split2(mat[...]))
    mean1 = row_dot(mean0, lead1) - last1
    mean2 = row_dot(mean0, lead2) - last2
    root_out[...] = mean0
    group_out[...] = mean1
    fine_out[...] = mean2

    def fit(mean, a):
        left = jnp.broadcast_to(mean, (16, R)).astype(BF)
        return dot(left, basis[a], NT)

    field_out[...] = (fit(mean0, 0) + fit(mean1, 1) + fit(mean2, 2))[0:1, :]
    grid1.wait_send(range(5))
    grid01.wait_send(range(4))
    grid0.wait_send(range(2))
    across.wait_send()
    early0.wait_send()
    gather0.wait_send()


def place_kernel(root, group, fine, field, root_out, group_out, fine_out, field_out):
    lanes = root_out.shape[1]
    first = lax.axis_index("sub") * lanes
    tile = pl.multiple_of(lax.div(first, 128) * 128, 128)
    shift = lax.rem(128 - (first - tile), 128)
    for whole, out in ((root, root_out), (group, group_out)):
        out[...] = pltpu.roll(jnp.broadcast_to(whole[:, pl.ds(tile, 128)], (8, 128)), shift, 1)[0:1, 0:lanes]
    fine_out[...] = fine[...]
    field_out[...] = field[...]


def shape(*dims):
    return jax.ShapeDtypeStruct(dims, F32)


def shards(basis, observations, counts, noise_prec, prior_fine, prior_group, prior_root):
    slots = basis.shape[1]
    nsub, ngrp = lax.axis_size("sub"), lax.axis_size("grp")

    def buf(*dims, kind=F32):
        return pltpu.VMEM(dims, kind)

    def halves(one, two, lanes):
        sizes = (one, two)
        return (
            [buf(SIDE, SIDE, size, lanes) for size in sizes] + [buf(SIDE, size, lanes) for size in sizes]
            + [buf(SIDE, size, lanes) for size in sizes]
        )

    root, group, fine, field = pl.pallas_call(
        kernel,
        name="levels",
        out_shape=[shape(1, R), shape(1, R), shape(1, R), shape(1, slots)],
        in_specs=[SM, SM, VM, HB, HB, HB, HB],
        out_specs=[VM] * 4,
        scratch_shapes=[
            buf(3, slots, R, kind=BF), buf(R, R), buf(128, 128), buf(R, R), buf(R, R), buf(AUG, R),
            buf(2 * R, R, kind=BF), buf(2 * R, R, kind=BF), buf(16, R),
            buf(R, R), buf(SIDE, SIDE, R // nsub, R), buf(R, R), buf(16, R), buf(16, R),
            buf(R, R), buf(SIDE, SIDE, R // nsub, R), buf(8, R), buf(8, R),
            buf(PIECE, 128), buf(ngrp, PIECE, 128), buf(SIDE, SIDE, PIECE, 128),
            [buf(SIDE, SIDE, PIECE, 128), *halves(CUT, PIECE - CUT, 128), buf(SIDE, SIDE, PIECE, 128)],
            halves(R // nsub // 2, R // nsub // 2, R),
            [buf(SIDE, SIDE, PIECE, 128), *halves(CUT, PIECE - CUT, 128)],
            pltpu.SemaphoreType.DMA((6,)),
            pltpu.SemaphoreType.DMA((3, 5, 2, SIDE)), pltpu.SemaphoreType.DMA((3, 5, 2, SIDE)),
            pltpu.SemaphoreType.DMA((2, nsub)), pltpu.SemaphoreType.DMA((2, nsub)),
            pltpu.SemaphoreType.DMA((ngrp,)), pltpu.SemaphoreType.DMA((ngrp,)),
        ],
        compiler_params=pltpu.CompilerParams(collective_id=0, has_side_effects=True, vmem_limit_bytes=60 << 20),
    )(counts, noise_prec, observations.reshape(slots // 128, 128), basis, prior_fine, prior_group, prior_root)
    outs = pl.pallas_call(
        place_kernel,
        name="place",
        out_shape=[shape(1, R // nsub), shape(1, R // nsub), shape(1, R), shape(1, slots)],
        in_specs=[VM] * 4,
        out_specs=[VM] * 4,
    )(root, group, fine, field)
    return tuple(out[0] for out in outs)


def solution(mesh):
    in_specs = (
        P(None, ("grp", "sub"), None),
        P(("grp", "sub")),
        P(("grp", "sub")),
        P(("grp", "sub")),
        P(("grp", "sub"), None, None),
        P("grp", None, None),
        P(),
    )
    out_specs = (P("sub"), P(("grp", "sub")), P(("grp", "sub")), P(("grp", "sub")))
    return jax.shard_map(shards, mesh=mesh, in_specs=in_specs, out_specs=out_specs, check_vma=False)
```

```python
import functools

import jax
import jax.numpy as jnp
from jax import lax
from jax.experimental import pallas as pl
from jax.experimental.pallas import tpu as pltpu
from jax.sharding import PartitionSpec as P

F32 = jnp.float32
BF = jnp.bfloat16
MESH = pl.DeviceIdType.MESH
R = 512
NB = 16
AUG = R + 16
VM = pl.BlockSpec(memory_space=pltpu.VMEM)
SM = pl.BlockSpec(memory_space=pltpu.SMEM)
HB = pl.BlockSpec(memory_space=pl.ANY)
NN = (((1,), (0,)), ((), ()))
TN = (((0,), (0,)), ((), ()))
NT = (((1,), (1,)), ((), ()))


def split2(x):
    high = x.astype(BF)
    return high, (x - high.astype(F32)).astype(BF)


def split3(x):
    high = x.astype(BF)
    rest = x - high.astype(F32)
    mid = rest.astype(BF)
    return high, mid, (rest - mid.astype(F32)).astype(BF)


def dot(left, right, dims):
    return lax.dot_general(left, right, dims, preferred_element_type=F32)


def dot3(left, right, dims):
    a, b = left if isinstance(left, tuple) else split2(left)
    c, d = right if isinstance(right, tuple) else split2(right)
    (k,), (m,) = dims[0]
    return dot(jnp.concatenate([a, a, b], k), jnp.concatenate([c, d, c], m), dims)


def splat_columns(rows, first, lane):
    return [
        jnp.broadcast_to(jnp.sum(jnp.where(lane == first + j, rows, 0.0), axis=1, keepdims=True), (NB, 128))
        for j in range(NB)
    ]


def eliminate(rows, first, sub, lane):
    inside = (lane >= first) & (lane < first + NB)
    eye = jnp.where(lane == first + sub, -1.0, 0.0)
    work = jnp.stack(splat_columns(rows, first, lane) + [jnp.where(inside, eye, rows)], 0)
    for i in range(NB):
        mine = sub[0:8] == i % 8
        inv = 1.0 / jnp.broadcast_to(work[0, i : i + 1, :], (8, 128))
        rest = work[1:]
        pivot_row = jnp.broadcast_to(rest[:, i : i + 1, :], (rest.shape[0], 8, 128))
        out = []
        for g in range(NB // 8):
            place = slice(8 * g, 8 * g + 8)
            base, mult = rest[:, place], -work[0, place] * inv
            if g == i // 8:
                base, mult = jnp.where(mine[None], 0.0, base), jnp.where(mine, inv, mult)
            out.append(base + mult[None] * pivot_row)
        work = jnp.concatenate(out, 1)
    return work[0]


def sweep_block(mat, halfway=None):
    count = 128 // NB
    sub = lax.broadcasted_iota(jnp.int32, (NB, 128), 0)
    lane = lax.broadcasted_iota(jnp.int32, (NB, 128), 1)

    def inside(p):
        return (lane >= p * NB) & (lane < p * NB + NB)

    def place(p):
        return pl.ds(pl.multiple_of(p * NB, NB), NB)

    def update(p, rows, panel):
        mat[...] = jnp.where(inside(p)[0:1], 0.0, mat[...]) - dot3(rows, panel, TN)
        mat[place(p), :] = panel

    def advance(following, p, panel):
        cols = splat_columns(following, p * NB, lane)
        terms = [cols[m] * jnp.broadcast_to(panel[m : m + 1, :], (NB, 128)) for m in range(NB)]
        while len(terms) > 1:
            terms = [terms[i] + terms[i + 1] for i in range(0, len(terms), 2)]
        return jnp.where(inside(p), 0.0, following) - terms[0]

    def body(p, carry):
        rows, before, panel_before = carry
        update(p - 1, before, panel_before)
        following = mat[place(jnp.minimum(p + 1, count - 1)), :]
        panel = eliminate(rows, p * NB, sub, lane)
        return advance(following, p, panel), rows, panel

    rows = mat[0:NB, :]
    panel = eliminate(rows, 0, sub, lane)
    start = (advance(mat[NB : 2 * NB, :], 0, panel), rows, panel)
    if halfway is not None:
        start = lax.fori_loop(1, count // 2, body, start)
        halfway()
    _, rows, panel = lax.fori_loop(1 if halfway is None else count // 2, count, body, start)
    update(count - 1, rows, panel)


def negative_inverse(mat, block, ready=None, half=(), inner=(), outer=()):
    n = mat.shape[0]
    if ready is None:
        block[...] = mat[0:128, 0:128]
    for k in range(n // 128):
        mine, after = slice(128 * k, 128 * k + 128), slice(128 * k + 128, 128 * k + 256)
        sweep_block(block, dict(half).get(k))
        if k in dict(inner):
            dict(inner)[k]()
        if k == 0 and ready is not None:
            ready()
        own = block[...]
        rows = split2(mat[mine, :])
        panel = -dot3(own, rows, NN)
        panel = jnp.concatenate(
            [own if c == k else panel[:, 128 * c : 128 * c + 128] for c in range(n // 128)], 1
        )
        parts = split2(panel)
        if k + 1 < n // 128:
            block[...] = mat[after, after] - dot3(
                tuple(part[:, after] for part in rows), tuple(part[:, after] for part in parts), TN
            )
        mat[:, mine] = jnp.zeros((n, 128), F32)
        mat[...] = mat[...] - dot3(rows, parts, TN)
        mat[mine, :] = panel
        if k in dict(outer):
            dict(outer)[k]()


def row_dot(vec, parts):
    a, b, c = [part.astype(F32) for part in split3(vec)]
    index = lax.broadcasted_iota(jnp.int32, (16, vec.shape[1]), 0)
    left = jnp.where(index == 0, a, jnp.where(index == 1, b, jnp.where(index == 2, c, 0.0))).astype(BF)
    out = dot(left, parts[0], NN) + dot(left, parts[1], NN)
    return jnp.sum(out, axis=0, keepdims=True)


SLAB = 16
TILES = R // 128
SYM = 5 * SLAB
PIECE = SYM + 8
CUT = 48
HALF = 8
SIDE = 4


def piece_tiles(group):
    low = group + 1
    return [(False, t) for t in range(low)] + [(True, t) for t in range(5 - low)]


def slab_rows(index):
    return pl.ds(pl.multiple_of(index * SLAB, SLAB), SLAB)


def pack(full, vec, pieces):
    pieces[:, :, SYM:PIECE, :] = jnp.zeros((SIDE, SIDE, 8, 128), F32)
    for group in range(2):

        def body(i, carry):
            s = group * HALF + i
            for t, (high, tile) in enumerate(piece_tiles(group)):
                rows = slab_rows(2 * SIDE * SIDE - 1 - s if high else s)
                pieces[lax.div(s, SIDE), lax.rem(s, SIDE), SLAB * t : SLAB * t + SLAB, :] = full[
                    rows, 128 * tile : 128 * tile + 128
                ]
            return carry

        lax.fori_loop(0, HALF, body, 0)
    for c in range(TILES):
        pieces[c, 0, SYM:PIECE, :] = vec[0:8, 128 * c : 128 * c + 128]


def unpack(pieces, full, vec, prior):
    for group in range(2):

        def body(i, carry):
            s = group * HALF + i
            for t, (high, tile) in enumerate(piece_tiles(group)):
                rows = slab_rows(2 * SIDE * SIDE - 1 - s if high else s)
                lanes = slice(128 * tile, 128 * tile + 128)
                part = pieces[lax.div(s, SIDE), lax.rem(s, SIDE), SLAB * t : SLAB * t + SLAB, :]
                full[rows, lanes] = part + prior[rows, lanes]
            return carry

        lax.fori_loop(0, HALF, body, 0)
    for i in range(TILES):
        for j in range(i):
            full[128 * j : 128 * j + 128, 128 * i : 128 * i + 128] = full[
                128 * i : 128 * i + 128, 128 * j : 128 * j + 128
            ].T
    for c in range(TILES):
        vec[0:8, 128 * c : 128 * c + 128] = pieces[c, 0, SYM:PIECE, :]


def first_block(pieces, prior, block):
    for s in range(HALF):
        rows = slice(SLAB * s, SLAB * s + SLAB)
        block[rows, :] = pieces[s // SIDE, s % SIDE, 0:SLAB, :] + prior[rows, 0:128]


class Exchange:
    def __init__(self, axis, source, into, send_sem, recv_sem):
        self.axis, self.source, self.into, self.send_sem, self.recv_sem = axis, source, into, send_sem, recv_sem
        self.n = lax.axis_size(axis)
        self.me = lax.axis_index(axis)

    def copy(self, d):
        peer = lax.rem(self.me + d, self.n)
        return pltpu.make_async_remote_copy(
            src_ref=self.source(peer),
            dst_ref=self.into(d),
            send_sem=self.send_sem.at[d],
            recv_sem=self.recv_sem.at[d],
            device_id={self.axis: peer},
            device_id_type=MESH,
        )

    def each(self, act):
        def body(d, carry):
            act(self.copy(d))
            return carry

        lax.fori_loop(1, self.n, body, 0)

    def start(self):
        self.each(lambda copy: copy.start())

    def wait_recv(self):
        self.each(lambda copy: copy.wait_recv())

    def wait_send(self):
        self.each(lambda copy: copy.wait_send())


class Grid:
    def __init__(self, source, cut, from_x, from_y, mid_x, mid_y, late_x, late_y, result, send_sem, recv_sem, early=0):
        self.source, self.cut, self.result = source, cut, result
        self.from_x, self.from_y, self.mid_x, self.mid_y = from_x, from_y, mid_x, mid_y
        self.late_x, self.late_y = late_x, late_y
        self.send_sem, self.recv_sem = send_sem, recv_sem
        sub = lax.axis_index("sub")
        self.px, self.py = lax.div(sub, SIDE), lax.rem(sub, SIDE)
        self.first, self.rest = slice(0, cut), slice(cut, source.shape[2])
        self.early = early

    def copies(self, phase):
        out = []
        px, py, first, rest = self.px, self.py, self.first, self.rest
        source, result = self.source, self.result
        for d in range(1, SIDE):
            x, y = lax.rem(px + d, SIDE), lax.rem(py + d, SIDE)
            at_x, at_y = x * SIDE + py, px * SIDE + y
            if phase == 0:
                pair = (
                    (source.at[x, :, first, :], self.from_x.at[d], at_x),
                    (source.at[:, y, rest, :], self.from_y.at[d], at_y),
                )
            elif phase == 1:
                pair = (
                    (self.mid_x.at[y], self.late_x.at[d], at_y),
                    (self.mid_y.at[x], self.late_y.at[d], at_x),
                )
            elif phase == 2:
                one, two = result.at[px, py, first, :], result.at[px, py, rest, :]
                pair = ((one, one, at_y), (two, two, at_x))
            elif phase == 3:
                one, two = result.at[px, :, self.early : self.cut, :], result.at[:, py, rest, :]
                pair = ((one, one, at_x), (two, two, at_y))
            else:
                one = result.at[px, :, 0 : self.early, :]
                pair = ((one, one, at_x),)
            for k, (src, dst, peer) in enumerate(pair):
                out.append(
                    pltpu.make_async_remote_copy(
                        src_ref=src,
                        dst_ref=dst,
                        send_sem=self.send_sem.at[phase, k, d],
                        recv_sem=self.recv_sem.at[phase, k, d],
                        device_id={"sub": peer},
                        device_id_type=MESH,
                    )
                )
        return out

    def start(self, phase):
        for copy in self.copies(phase):
            copy.start()

    def wait_recv(self, phase):
        for copy in self.copies(phase):
            copy.wait_recv()

    def wait_send(self, phases):
        for phase in phases:
            for copy in self.copies(phase):
                copy.wait_send()

    def middle(self):
        self.mid_x[...] = self.source[self.px, :, self.first, :] + jnp.sum(self.from_x[1:], axis=0)
        self.mid_y[...] = self.source[:, self.py, self.rest, :] + jnp.sum(self.from_y[1:], axis=0)

    def finish(self, target):
        target[self.first, :] = self.mid_x[self.py] + jnp.sum(self.late_x[1:], axis=0)
        target[self.rest, :] = self.mid_y[self.px] + jnp.sum(self.late_y[1:], axis=0)


def first_row(vec, rows):
    total = jnp.sum(vec, axis=0, keepdims=True)
    index = lax.broadcasted_iota(jnp.int32, (rows, vec.shape[1]), 0)
    return jnp.where(index == 0, total, 0.0)


def kernel(
    count, tau, obs, basis_hbm, fine_hbm, group_hbm, root_hbm,
    root_out, group_out, fine_out, field_out,
    basis, mat, block, prior1, prior0, cross, high, low, xvec, s11, s01, s00, vec1, vec0, inv1, a01, a1, b0,
    mid0, recvg, all0, bufs1, bufs01, bufs0, load_sem, sem_s, sem_r, sema_s, sema_r, semg_s, semg_r,
):
    sub = lax.axis_index("sub")
    grp = lax.axis_index("grp")
    nsub, ngrp = lax.axis_size("sub"), lax.axis_size("grp")
    rows = R // nsub

    def load(k):
        pairs = (
            (basis_hbm.at[2], basis.at[2]), (fine_hbm.at[0], mat), (basis_hbm.at[1], basis.at[1]),
            (basis_hbm.at[0], basis.at[0]), (group_hbm.at[0], prior1), (root_hbm, prior0),
        )
        return pltpu.make_async_copy(pairs[k][0], pairs[k][1], load_sem.at[k])

    for k in range(6):
        load(k).start()
    barrier = pltpu.get_barrier_semaphore()

    def greet(axis, me, n):
        def body(d, carry):
            pl.semaphore_signal(
                barrier, inc=1, device_id={axis: lax.rem(me + d, n)}, device_id_type=MESH
            )
            return carry

        lax.fori_loop(1, n, body, 0)

    greet("sub", sub, nsub)
    greet("grp", grp, ngrp)

    px, py = lax.div(sub, SIDE), lax.rem(sub, SIDE)
    send1, all1 = bufs1[0], bufs1[7]
    grid1 = Grid(send1, CUT, *bufs1[1:], sem_s.at[0], sem_r.at[0], early=SLAB)
    grid01 = Grid(s01, rows // 2, *bufs01, a01, sem_s.at[1], sem_r.at[1])
    send0 = bufs0[0]
    grid0 = Grid(send0, CUT, *bufs0[1:], None, sem_s.at[2], sem_r.at[2])
    tile0, tiles0 = all0.at[px, py, 0:SLAB, :], all0.at[px, py, SLAB:PIECE, :]
    early0 = Exchange("sub", lambda peer: tile0, lambda d: tile0, sema_s.at[0], sema_r.at[0])
    gather0 = Exchange("sub", lambda peer: tiles0, lambda d: tiles0, sema_s.at[1], sema_r.at[1])
    across = Exchange("grp", lambda peer: mid0, lambda d: recvg.at[d], semg_s, semg_r)

    slots = basis.shape[1]
    t = tau[0]
    n = count[0]
    valid = lax.broadcasted_iota(jnp.int32, (slots, 1), 0) < n
    chunks = slots // 128
    index = lax.broadcasted_iota(jnp.int32, (chunks, 128), 0)
    slot = index * 128 + lax.broadcasted_iota(jnp.int32, (chunks, 128), 1)
    y = jnp.where(slot < n, obs[...].astype(F32), 0.0)
    y = jnp.concatenate([jnp.where(index == c, y, 0.0) for c in range(chunks)], 1).astype(BF)

    def masked(a):
        block = basis[a]
        return jnp.where(valid, block, jnp.zeros_like(block))

    load(0).wait()
    m2 = masked(2)
    load(1).wait()
    mat[...] = mat[...] + t * dot(basis[2], m2, TN)
    cross[R:AUG, :] = first_row(t * dot(y, basis[2], NN), 16)
    load(2).wait()
    cross[0:R, :] = t * dot(basis[1], m2, TN)
    m1 = masked(1)
    s11[...] = t * dot(basis[1], m1, TN)
    vec1[...] = first_row(t * dot(y, basis[1], NN), 16)
    negative_inverse(mat, block)

    inv = split2(mat[...])
    cy = split2(cross[0:AUG, :])
    c1 = tuple(part[0:R] for part in cy)
    x1 = dot3(cy, inv, NN)
    xvec[...] = x1[R:AUG]
    x1 = split2(x1)
    high[0:R, :], low[0:R, :] = x1[0][0:R], x1[1][0:R]
    xy = tuple(part[R:AUG] for part in x1)
    add = dot3(x1, c1, NT)
    s11[...] = s11[...] + add[0:R]
    vec1[...] = vec1[...] + add[R:AUG]
    pack(s11, vec1, send1)
    pl.semaphore_wait(barrier, nsub + ngrp - 2)
    grid1.start(0)

    load(3).wait()
    m0 = masked(0)
    c0 = split2(t * dot(m0, basis[2], TN))
    x0 = split2(dot3(c0, inv, NN))
    high[R : 2 * R, :], low[R : 2 * R, :] = x0
    s01[...] = (t * dot(m0, basis[1], TN) + dot3(x0, c1, NT)).reshape(SIDE, SIDE, rows, R)
    grid01.start(0)
    grid1.wait_recv(0)
    grid1.middle()
    grid1.start(1)
    s00[...] = t * dot(m0, basis[0], TN) + dot3(x0, c0, NT)
    vec0[...] = first_row(t * dot(y, basis[0], NN), 16) + dot3(xy, c0, NT)
    pack(s00, vec0, send0)
    grid1.wait_recv(1)
    grid1.finish(all1.at[px, py])
    grid1.start(2)
    grid01.wait_recv(0)
    grid01.middle()
    grid01.start(1)
    grid1.wait_recv(2)
    grid1.start(4)
    grid1.start(3)
    grid01.wait_recv(1)
    grid01.finish(a01.at[px, py])
    grid01.start(2)
    load(4).wait()
    grid1.wait_recv(4)
    first_block(all1, prior1, block)

    def ready1():
        grid1.wait_recv(3)
        unpack(all1, inv1, a1, prior1)

    def one():
        grid01.wait_recv(2)
        grid01.start(3)

    def three():
        grid0.wait_recv(0)
        grid0.middle()
        grid0.start(1)

    negative_inverse(inv1, block, ready1, half=((0, one),), inner=((0, lambda: grid0.start(0)), (2, three)))
    grid0.wait_recv(1)
    grid0.finish(mid0)
    grid01.wait_recv(3)

    inv = split2(inv1[...])
    both = split2(a01[...].reshape(R, R))
    mine, mirror = lax.div(sub, 2), lax.div(2 * nsub - 1 - sub, 2)
    half = pl.multiple_of(lax.rem(sub, 2) * SLAB, SLAB)
    left = jnp.concatenate(
        [
            a01[lax.div(mine, SIDE), lax.rem(mine, SIDE), pl.ds(half, SLAB), :],
            a01[lax.div(mirror, SIDE), lax.rem(mirror, SIDE), pl.ds(pl.multiple_of(SLAB - half, SLAB), SLAB), :],
            a1[...], jnp.zeros((8, R), F32),
        ],
        0,
    )
    left = dot3(left, inv, NN)
    term = dot3(left, both, NT)
    upper = sub >= HALF
    for k, (one, two) in enumerate(zip(piece_tiles(0), piece_tiles(1))):
        parts = [
            term[SLAB * hi : SLAB * hi + SLAB, 128 * tile : 128 * tile + 128] for hi, tile in (one, two)
        ]
        place = slice(SLAB * k, SLAB * k + SLAB)
        mid0[place, :] = mid0[place, :] + jnp.where(upper, parts[1], parts[0])
    extra = jnp.zeros((8, 128), F32)
    for c in range(TILES):
        extra = extra + jnp.where(sub == 4 * c, term[2 * SLAB : 2 * SLAB + 8, 128 * c : 128 * c + 128], 0.0)
    mid0[SYM:PIECE, :] = mid0[SYM:PIECE, :] + extra
    across.start()
    lead1 = split2(dot3(both, inv, NN))
    last1 = left[2 * SLAB : 2 * SLAB + 1, :]
    fine1 = (high[0:R, :], low[0:R, :])
    across.wait_recv()
    recvg[0] = mid0[...]
    total = recvg[grp]
    for g in range(1, ngrp):
        total = total + recvg[lax.rem(grp - g + ngrp, ngrp)]
    all0[px, py] = total
    early0.start()
    gather0.start()
    lead2 = split2(high[R : 2 * R, :].astype(F32) + low[R : 2 * R, :].astype(F32) + dot3(lead1, fine1, NN))
    last2 = xvec[0:1, :] + row_dot(last1, fine1)
    load(5).wait()
    early0.wait_recv()
    first_block(all0, prior0, block)

    def ready0():
        gather0.wait_recv()
        unpack(all0, mat, b0, prior0)

    negative_inverse(mat, block, ready0)
    mean0 = -row_dot(b0[0:1, :], split2(mat[...]))
    mean1 = row_dot(mean0, lead1) - last1
    mean2 = row_dot(mean0, lead2) - last2
    root_out[...] = mean0
    group_out[...] = mean1
    fine_out[...] = mean2

    def fit(mean, a):
        left = jnp.broadcast_to(mean, (16, R)).astype(BF)
        return dot(left, basis[a], NT)

    field_out[...] = (fit(mean0, 0) + fit(mean1, 1) + fit(mean2, 2))[0:1, :]
    grid1.wait_send(range(5))
    grid01.wait_send(range(4))
    grid0.wait_send(range(2))
    across.wait_send()
    early0.wait_send()
    gather0.wait_send()


def place_kernel(root, group, fine, field, root_out, group_out, fine_out, field_out):
    lanes = root_out.shape[1]
    first = lax.axis_index("sub") * lanes
    tile = pl.multiple_of(lax.div(first, 128) * 128, 128)
    shift = lax.rem(128 - (first - tile), 128)
    for whole, out in ((root, root_out), (group, group_out)):
        out[...] = pltpu.roll(jnp.broadcast_to(whole[:, pl.ds(tile, 128)], (8, 128)), shift, 1)[0:1, 0:lanes]
    fine_out[...] = fine[...]
    field_out[...] = field[...]


def shape(*dims):
    return jax.ShapeDtypeStruct(dims, F32)


def shards(basis, observations, counts, noise_prec, prior_fine, prior_group, prior_root):
    slots = basis.shape[1]
    nsub, ngrp = lax.axis_size("sub"), lax.axis_size("grp")

    def buf(*dims, kind=F32):
        return pltpu.VMEM(dims, kind)

    def halves(one, two, lanes):
        sizes = (one, two)
        return (
            [buf(SIDE, SIDE, size, lanes) for size in sizes] + [buf(SIDE, size, lanes) for size in sizes]
            + [buf(SIDE, size, lanes) for size in sizes]
        )

    root, group, fine, field = pl.pallas_call(
        kernel,
        name="levels",
        out_shape=[shape(1, R), shape(1, R), shape(1, R), shape(1, slots)],
        in_specs=[SM, SM, VM, HB, HB, HB, HB],
        out_specs=[VM] * 4,
        scratch_shapes=[
            buf(3, slots, R, kind=BF), buf(R, R), buf(128, 128), buf(R, R), buf(R, R), buf(AUG, R),
            buf(2 * R, R, kind=BF), buf(2 * R, R, kind=BF), buf(16, R),
            buf(R, R), buf(SIDE, SIDE, R // nsub, R), buf(R, R), buf(16, R), buf(16, R),
            buf(R, R), buf(SIDE, SIDE, R // nsub, R), buf(8, R), buf(8, R),
            buf(PIECE, 128), buf(ngrp, PIECE, 128), buf(SIDE, SIDE, PIECE, 128),
            [buf(SIDE, SIDE, PIECE, 128), *halves(CUT, PIECE - CUT, 128), buf(SIDE, SIDE, PIECE, 128)],
            halves(R // nsub // 2, R // nsub // 2, R),
            [buf(SIDE, SIDE, PIECE, 128), *halves(CUT, PIECE - CUT, 128)],
            pltpu.SemaphoreType.DMA((6,)),
            pltpu.SemaphoreType.DMA((3, 5, 2, SIDE)), pltpu.SemaphoreType.DMA((3, 5, 2, SIDE)),
            pltpu.SemaphoreType.DMA((2, nsub)), pltpu.SemaphoreType.DMA((2, nsub)),
            pltpu.SemaphoreType.DMA((ngrp,)), pltpu.SemaphoreType.DMA((ngrp,)),
        ],
        compiler_params=pltpu.CompilerParams(collective_id=0, has_side_effects=True, vmem_limit_bytes=60 << 20),
    )(counts, noise_prec, observations.reshape(slots // 128, 128), basis, prior_fine, prior_group, prior_root)
    outs = pl.pallas_call(
        place_kernel,
        name="place",
        out_shape=[shape(1, R // nsub), shape(1, R // nsub), shape(1, R), shape(1, slots)],
        in_specs=[VM] * 4,
        out_specs=[VM] * 4,
    )(root, group, fine, field)
    return tuple(out[0] for out in outs)


def solution(mesh):
    in_specs = (
        P(None, ("grp", "sub"), None),
        P(("grp", "sub")),
        P(("grp", "sub")),
        P(("grp", "sub")),
        P(("grp", "sub"), None, None),
        P("grp", None, None),
        P(),
    )
    out_specs = (P("sub"), P(("grp", "sub")), P(("grp", "sub")), P(("grp", "sub")))
    return jax.shard_map(shards, mesh=mesh, in_specs=in_specs, out_specs=out_specs, check_vma=False)
```

```python
import functools

import jax
import jax.numpy as jnp
from jax import lax
from jax.experimental import pallas as pl
from jax.experimental.pallas import tpu as pltpu
from jax.sharding import PartitionSpec as P

F32 = jnp.float32
BF = jnp.bfloat16
MESH = pl.DeviceIdType.MESH
R = 512
NB = 16
AUG = R + 16
VM = pl.BlockSpec(memory_space=pltpu.VMEM)
SM = pl.BlockSpec(memory_space=pltpu.SMEM)
HB = pl.BlockSpec(memory_space=pl.ANY)
NN = (((1,), (0,)), ((), ()))
TN = (((0,), (0,)), ((), ()))
NT = (((1,), (1,)), ((), ()))


def split2(x):
    high = x.astype(BF)
    return high, (x - high.astype(F32)).astype(BF)


def split3(x):
    high = x.astype(BF)
    rest = x - high.astype(F32)
    mid = rest.astype(BF)
    return high, mid, (rest - mid.astype(F32)).astype(BF)


def dot(left, right, dims):
    return lax.dot_general(left, right, dims, preferred_element_type=F32)


def dot3(left, right, dims):
    a, b = left if isinstance(left, tuple) else split2(left)
    c, d = right if isinstance(right, tuple) else split2(right)
    (k,), (m,) = dims[0]
    return dot(jnp.concatenate([a, a, b], k), jnp.concatenate([c, d, c], m), dims)


def splat_columns(rows, first, lane):
    return [
        jnp.broadcast_to(jnp.sum(jnp.where(lane == first + j, rows, 0.0), axis=1, keepdims=True), (NB, 128))
        for j in range(NB)
    ]


def eliminate(rows, first, sub, lane):
    inside = (lane >= first) & (lane < first + NB)
    eye = jnp.where(lane == first + sub, -1.0, 0.0)
    work = jnp.stack(splat_columns(rows, first, lane) + [jnp.where(inside, eye, rows)], 0)
    for i in range(NB):
        mine = sub[0:8] == i % 8
        inv = 1.0 / jnp.broadcast_to(work[0, i : i + 1, :], (8, 128))
        rest = work[1:]
        pivot_row = jnp.broadcast_to(rest[:, i : i + 1, :], (rest.shape[0], 8, 128))
        out = []
        for g in range(NB // 8):
            place = slice(8 * g, 8 * g + 8)
            base, mult = rest[:, place], -work[0, place] * inv
            if g == i // 8:
                base, mult = jnp.where(mine[None], 0.0, base), jnp.where(mine, inv, mult)
            out.append(base + mult[None] * pivot_row)
        work = jnp.concatenate(out, 1)
    return work[0]


def sweep_block(mat, halfway=None):
    count = 128 // NB
    sub = lax.broadcasted_iota(jnp.int32, (NB, 128), 0)
    lane = lax.broadcasted_iota(jnp.int32, (NB, 128), 1)

    def inside(p):
        return (lane >= p * NB) & (lane < p * NB + NB)

    def place(p):
        return pl.ds(pl.multiple_of(p * NB, NB), NB)

    def update(p, rows, panel):
        mat[...] = jnp.where(inside(p)[0:1], 0.0, mat[...]) - dot3(rows, panel, TN)
        mat[place(p), :] = panel

    def advance(following, p, panel):
        cols = splat_columns(following, p * NB, lane)
        terms = [cols[m] * jnp.broadcast_to(panel[m : m + 1, :], (NB, 128)) for m in range(NB)]
        while len(terms) > 1:
            terms = [terms[i] + terms[i + 1] for i in range(0, len(terms), 2)]
        return jnp.where(inside(p), 0.0, following) - terms[0]

    def body(p, carry):
        rows, before, panel_before = carry
        update(p - 1, before, panel_before)
        following = mat[place(jnp.minimum(p + 1, count - 1)), :]
        panel = eliminate(rows, p * NB, sub, lane)
        return advance(following, p, panel), rows, panel

    rows = mat[0:NB, :]
    panel = eliminate(rows, 0, sub, lane)
    start = (advance(mat[NB : 2 * NB, :], 0, panel), rows, panel)
    if halfway is not None:
        start = lax.fori_loop(1, count // 2, body, start)
        halfway()
    _, rows, panel = lax.fori_loop(1 if halfway is None else count // 2, count, body, start)
    update(count - 1, rows, panel)


def negative_inverse(mat, block, ready=None, half=(), inner=(), outer=()):
    n = mat.shape[0]
    if ready is None:
        block[...] = mat[0:128, 0:128]
    for k in range(n // 128):
        mine, after = slice(128 * k, 128 * k + 128), slice(128 * k + 128, 128 * k + 256)
        sweep_block(block, dict(half).get(k))
        if k in dict(inner):
            dict(inner)[k]()
        if k == 0 and ready is not None:
            ready()
        own = block[...]
        rows = split2(mat[mine, :])
        panel = -dot3(own, rows, NN)
        panel = jnp.concatenate(
            [own if c == k else panel[:, 128 * c : 128 * c + 128] for c in range(n // 128)], 1
        )
        parts = split2(panel)
        if k + 1 < n // 128:
            block[...] = mat[after, after] - dot3(
                tuple(part[:, after] for part in rows), tuple(part[:, after] for part in parts), TN
            )
        mat[:, mine] = jnp.zeros((n, 128), F32)
        mat[...] = mat[...] - dot3(rows, parts, TN)
        mat[mine, :] = panel
        if k in dict(outer):
            dict(outer)[k]()


def row_dot(vec, parts):
    a, b, c = [part.astype(F32) for part in split3(vec)]
    index = lax.broadcasted_iota(jnp.int32, (16, vec.shape[1]), 0)
    left = jnp.where(index == 0, a, jnp.where(index == 1, b, jnp.where(index == 2, c, 0.0))).astype(BF)
    out = dot(left, parts[0], NN) + dot(left, parts[1], NN)
    return jnp.sum(out, axis=0, keepdims=True)


SLAB = 16
TILES = R // 128
SYM = 5 * SLAB
PIECE = SYM + 8
CUT = 48
HALF = 8
SIDE = 4


def piece_tiles(group):
    low = group + 1
    return [(False, t) for t in range(low)] + [(True, t) for t in range(5 - low)]


def slab_rows(index):
    return pl.ds(pl.multiple_of(index * SLAB, SLAB), SLAB)


def pack(full, vec, pieces):
    pieces[:, :, SYM:PIECE, :] = jnp.zeros((SIDE, SIDE, 8, 128), F32)
    for group in range(2):

        def body(i, carry):
            s = group * HALF + i
            for t, (high, tile) in enumerate(piece_tiles(group)):
                rows = slab_rows(2 * SIDE * SIDE - 1 - s if high else s)
                pieces[lax.div(s, SIDE), lax.rem(s, SIDE), SLAB * t : SLAB * t + SLAB, :] = full[
                    rows, 128 * tile : 128 * tile + 128
                ]
            return carry

        lax.fori_loop(0, HALF, body, 0)
    for c in range(TILES):
        pieces[c, 0, SYM:PIECE, :] = vec[0:8, 128 * c : 128 * c + 128]


def unpack(pieces, full, vec, prior):
    for group in range(2):

        def body(i, carry):
            s = group * HALF + i
            for t, (high, tile) in enumerate(piece_tiles(group)):
                rows = slab_rows(2 * SIDE * SIDE - 1 - s if high else s)
                lanes = slice(128 * tile, 128 * tile + 128)
                part = pieces[lax.div(s, SIDE), lax.rem(s, SIDE), SLAB * t : SLAB * t + SLAB, :]
                full[rows, lanes] = part + prior[rows, lanes]
            return carry

        lax.fori_loop(0, HALF, body, 0)
    for i in range(TILES):
        for j in range(i):
            full[128 * j : 128 * j + 128, 128 * i : 128 * i + 128] = full[
                128 * i : 128 * i + 128, 128 * j : 128 * j + 128
            ].T
    for c in range(TILES):
        vec[0:8, 128 * c : 128 * c + 128] = pieces[c, 0, SYM:PIECE, :]


def first_block(pieces, prior, block):
    for s in range(HALF):
        rows = slice(SLAB * s, SLAB * s + SLAB)
        block[rows, :] = pieces[s // SIDE, s % SIDE, 0:SLAB, :] + prior[rows, 0:128]


class Exchange:
    def __init__(self, axis, source, into, send_sem, recv_sem):
        self.axis, self.source, self.into, self.send_sem, self.recv_sem = axis, source, into, send_sem, recv_sem
        self.n = lax.axis_size(axis)
        self.me = lax.axis_index(axis)

    def copy(self, d):
        peer = lax.rem(self.me + d, self.n)
        return pltpu.make_async_remote_copy(
            src_ref=self.source(peer),
            dst_ref=self.into(d),
            send_sem=self.send_sem.at[d],
            recv_sem=self.recv_sem.at[d],
            device_id={self.axis: peer},
            device_id_type=MESH,
        )

    def each(self, act):
        def body(d, carry):
            act(self.copy(d))
            return carry

        lax.fori_loop(1, self.n, body, 0)

    def start(self):
        self.each(lambda copy: copy.start())

    def wait_recv(self):
        self.each(lambda copy: copy.wait_recv())

    def wait_send(self):
        self.each(lambda copy: copy.wait_send())


class Grid:
    def __init__(self, source, cut, from_x, from_y, mid_x, mid_y, late_x, late_y, result, send_sem, recv_sem, early=0):
        self.source, self.cut, self.result = source, cut, result
        self.from_x, self.from_y, self.mid_x, self.mid_y = from_x, from_y, mid_x, mid_y
        self.late_x, self.late_y = late_x, late_y
        self.send_sem, self.recv_sem = send_sem, recv_sem
        sub = lax.axis_index("sub")
        self.px, self.py = lax.div(sub, SIDE), lax.rem(sub, SIDE)
        self.first, self.rest = slice(0, cut), slice(cut, source.shape[2])
        self.early = early

    def copies(self, phase):
        out = []
        px, py, first, rest = self.px, self.py, self.first, self.rest
        source, result = self.source, self.result
        for d in range(1, SIDE):
            x, y = lax.rem(px + d, SIDE), lax.rem(py + d, SIDE)
            at_x, at_y = x * SIDE + py, px * SIDE + y
            if phase == 0:
                pair = (
                    (source.at[x, :, first, :], self.from_x.at[d], at_x),
                    (source.at[:, y, rest, :], self.from_y.at[d], at_y),
                )
            elif phase == 1:
                pair = (
                    (self.mid_x.at[y], self.late_x.at[d], at_y),
                    (self.mid_y.at[x], self.late_y.at[d], at_x),
                )
            elif phase == 2:
                one, two = result.at[px, py, first, :], result.at[px, py, rest, :]
                pair = ((one, one, at_y), (two, two, at_x))
            elif phase == 3:
                one, two = result.at[px, :, self.early : self.cut, :], result.at[:, py, rest, :]
                pair = ((one, one, at_x), (two, two, at_y))
            else:
                one = result.at[px, :, 0 : self.early, :]
                pair = ((one, one, at_x),)
            for k, (src, dst, peer) in enumerate(pair):
                out.append(
                    pltpu.make_async_remote_copy(
                        src_ref=src,
                        dst_ref=dst,
                        send_sem=self.send_sem.at[phase, k, d],
                        recv_sem=self.recv_sem.at[phase, k, d],
                        device_id={"sub": peer},
                        device_id_type=MESH,
                    )
                )
        return out

    def start(self, phase):
        for copy in self.copies(phase):
            copy.start()

    def wait_recv(self, phase):
        for copy in self.copies(phase):
            copy.wait_recv()

    def wait_send(self, phases):
        for phase in phases:
            for copy in self.copies(phase):
                copy.wait_send()

    def middle(self):
        self.mid_x[...] = self.source[self.px, :, self.first, :] + jnp.sum(self.from_x[1:], axis=0)
        self.mid_y[...] = self.source[:, self.py, self.rest, :] + jnp.sum(self.from_y[1:], axis=0)

    def finish(self, target):
        target[self.first, :] = self.mid_x[self.py] + jnp.sum(self.late_x[1:], axis=0)
        target[self.rest, :] = self.mid_y[self.px] + jnp.sum(self.late_y[1:], axis=0)


def first_row(vec, rows):
    total = jnp.sum(vec, axis=0, keepdims=True)
    index = lax.broadcasted_iota(jnp.int32, (rows, vec.shape[1]), 0)
    return jnp.where(index == 0, total, 0.0)


def kernel(
    count, tau, obs, basis_hbm, fine_hbm, group_hbm, root_hbm,
    root_out, group_out, fine_out, field_out,
    basis, mat, block, prior1, prior0, cross, high, low, xvec, s11, s01, s00, vec1, vec0, inv1, a01, a1, b0,
    mid0, recvg, all0, bufs1, bufs01, bufs0, load_sem, sem_s, sem_r, sema_s, sema_r, semg_s, semg_r,
):
    sub = lax.axis_index("sub")
    grp = lax.axis_index("grp")
    nsub, ngrp = lax.axis_size("sub"), lax.axis_size("grp")
    rows = R // nsub

    part = basis.shape[1] // 2

    def load(k):
        pairs = (
            (basis_hbm.at[2, 0:part], basis.at[2, 0:part]), (fine_hbm.at[0], mat), (basis_hbm.at[1], basis.at[1]),
            (basis_hbm.at[0], basis.at[0]), (group_hbm.at[0], prior1), (root_hbm, prior0),
            (basis_hbm.at[2, part:], basis.at[2, part:]),
        )
        return pltpu.make_async_copy(pairs[k][0], pairs[k][1], load_sem.at[k])

    for k in (0, 6, 1, 2, 3, 4, 5):
        load(k).start()
    barrier = pltpu.get_barrier_semaphore()

    def greet(axis, me, n):
        def body(d, carry):
            pl.semaphore_signal(
                barrier, inc=1, device_id={axis: lax.rem(me + d, n)}, device_id_type=MESH
            )
            return carry

        lax.fori_loop(1, n, body, 0)

    greet("sub", sub, nsub)
    greet("grp", grp, ngrp)

    px, py = lax.div(sub, SIDE), lax.rem(sub, SIDE)
    send1, all1 = bufs1[0], bufs1[7]
    grid1 = Grid(send1, CUT, *bufs1[1:], sem_s.at[0], sem_r.at[0], early=SLAB)
    grid01 = Grid(s01, rows // 2, *bufs01, a01, sem_s.at[1], sem_r.at[1])
    send0 = bufs0[0]
    grid0 = Grid(send0, CUT, *bufs0[1:], None, sem_s.at[2], sem_r.at[2])
    tile0, tiles0 = all0.at[px, py, 0:SLAB, :], all0.at[px, py, SLAB:PIECE, :]
    early0 = Exchange("sub", lambda peer: tile0, lambda d: tile0, sema_s.at[0], sema_r.at[0])
    gather0 = Exchange("sub", lambda peer: tiles0, lambda d: tiles0, sema_s.at[1], sema_r.at[1])
    across = Exchange("grp", lambda peer: mid0, lambda d: recvg.at[d], semg_s, semg_r)

    slots = basis.shape[1]
    t = tau[0]
    n = count[0]
    valid = lax.broadcasted_iota(jnp.int32, (slots, 1), 0) < n
    chunks = slots // 128
    index = lax.broadcasted_iota(jnp.int32, (chunks, 128), 0)
    slot = index * 128 + lax.broadcasted_iota(jnp.int32, (chunks, 128), 1)
    y = jnp.where(slot < n, obs[...].astype(F32), 0.0)
    y = jnp.concatenate([jnp.where(index == c, y, 0.0) for c in range(chunks)], 1).astype(BF)

    def masked(a):
        block = basis[a]
        return jnp.where(valid, block, jnp.zeros_like(block))

    load(0).wait()
    load(6).wait()
    m2 = masked(2)
    load(1).wait()
    mat[...] = mat[...] + t * dot(basis[2], m2, TN)
    cross[R:AUG, :] = first_row(t * dot(y, basis[2], NN), 16)
    load(2).wait()
    cross[0:R, :] = t * dot(basis[1], m2, TN)
    m1 = masked(1)
    s11[...] = t * dot(basis[1], m1, TN)
    vec1[...] = first_row(t * dot(y, basis[1], NN), 16)
    negative_inverse(mat, block)

    inv = split2(mat[...])
    cy = split2(cross[0:AUG, :])
    c1 = tuple(part[0:R] for part in cy)
    x1 = dot3(cy, inv, NN)
    xvec[...] = x1[R:AUG]
    x1 = split2(x1)
    high[0:R, :], low[0:R, :] = x1[0][0:R], x1[1][0:R]
    xy = tuple(part[R:AUG] for part in x1)
    add = dot3(x1, c1, NT)
    s11[...] = s11[...] + add[0:R]
    vec1[...] = vec1[...] + add[R:AUG]
    pack(s11, vec1, send1)
    pl.semaphore_wait(barrier, nsub + ngrp - 2)
    grid1.start(0)

    load(3).wait()
    m0 = masked(0)
    c0 = split2(t * dot(m0, basis[2], TN))
    x0 = split2(dot3(c0, inv, NN))
    high[R : 2 * R, :], low[R : 2 * R, :] = x0
    s01[...] = (t * dot(m0, basis[1], TN) + dot3(x0, c1, NT)).reshape(SIDE, SIDE, rows, R)
    grid01.start(0)
    grid1.wait_recv(0)
    grid1.middle()
    grid1.start(1)
    s00[...] = t * dot(m0, basis[0], TN) + dot3(x0, c0, NT)
    vec0[...] = first_row(t * dot(y, basis[0], NN), 16) + dot3(xy, c0, NT)
    pack(s00, vec0, send0)
    grid1.wait_recv(1)
    grid1.finish(all1.at[px, py])
    grid1.start(2)
    grid01.wait_recv(0)
    grid01.middle()
    grid01.start(1)
    grid1.wait_recv(2)
    grid1.start(4)
    grid1.start(3)
    grid01.wait_recv(1)
    grid01.finish(a01.at[px, py])
    grid01.start(2)
    load(4).wait()
    grid1.wait_recv(4)
    first_block(all1, prior1, block)

    def ready1():
        grid1.wait_recv(3)
        unpack(all1, inv1, a1, prior1)

    def one():
        grid01.wait_recv(2)
        grid01.start(3)

    def three():
        grid0.wait_recv(0)
        grid0.middle()
        grid0.start(1)

    negative_inverse(inv1, block, ready1, half=((0, one),), inner=((0, lambda: grid0.start(0)), (2, three)))
    grid0.wait_recv(1)
    grid0.finish(mid0)
    grid01.wait_recv(3)

    inv = split2(inv1[...])
    both = split2(a01[...].reshape(R, R))
    mine, mirror = lax.div(sub, 2), lax.div(2 * nsub - 1 - sub, 2)
    half = pl.multiple_of(lax.rem(sub, 2) * SLAB, SLAB)
    left = jnp.concatenate(
        [
            a01[lax.div(mine, SIDE), lax.rem(mine, SIDE), pl.ds(half, SLAB), :],
            a01[lax.div(mirror, SIDE), lax.rem(mirror, SIDE), pl.ds(pl.multiple_of(SLAB - half, SLAB), SLAB), :],
            a1[...], jnp.zeros((8, R), F32),
        ],
        0,
    )
    left = dot3(left, inv, NN)
    term = dot3(left, both, NT)
    upper = sub >= HALF
    for k, (one, two) in enumerate(zip(piece_tiles(0), piece_tiles(1))):
        parts = [
            term[SLAB * hi : SLAB * hi + SLAB, 128 * tile : 128 * tile + 128] for hi, tile in (one, two)
        ]
        place = slice(SLAB * k, SLAB * k + SLAB)
        mid0[place, :] = mid0[place, :] + jnp.where(upper, parts[1], parts[0])
    extra = jnp.zeros((8, 128), F32)
    for c in range(TILES):
        extra = extra + jnp.where(sub == 4 * c, term[2 * SLAB : 2 * SLAB + 8, 128 * c : 128 * c + 128], 0.0)
    mid0[SYM:PIECE, :] = mid0[SYM:PIECE, :] + extra
    across.start()
    lead1 = split2(dot3(both, inv, NN))
    last1 = left[2 * SLAB : 2 * SLAB + 1, :]
    fine1 = (high[0:R, :], low[0:R, :])
    across.wait_recv()
    recvg[0] = mid0[...]
    total = recvg[grp]
    for g in range(1, ngrp):
        total = total + recvg[lax.rem(grp - g + ngrp, ngrp)]
    all0[px, py] = total
    early0.start()
    gather0.start()
    lead2 = split2(high[R : 2 * R, :].astype(F32) + low[R : 2 * R, :].astype(F32) + dot3(lead1, fine1, NN))
    last2 = xvec[0:1, :] + row_dot(last1, fine1)
    load(5).wait()
    early0.wait_recv()
    first_block(all0, prior0, block)

    def ready0():
        gather0.wait_recv()
        unpack(all0, mat, b0, prior0)

    negative_inverse(mat, block, ready0)
    mean0 = -row_dot(b0[0:1, :], split2(mat[...]))
    mean1 = row_dot(mean0, lead1) - last1
    mean2 = row_dot(mean0, lead2) - last2
    root_out[...] = mean0
    group_out[...] = mean1
    fine_out[...] = mean2

    def fit(mean, a):
        left = jnp.broadcast_to(mean, (16, R)).astype(BF)
        return dot(left, basis[a], NT)

    field_out[...] = (fit(mean0, 0) + fit(mean1, 1) + fit(mean2, 2))[0:1, :]
    grid1.wait_send(range(5))
    grid01.wait_send(range(4))
    grid0.wait_send(range(2))
    across.wait_send()
    early0.wait_send()
    gather0.wait_send()


def place_kernel(root, group, fine, field, root_out, group_out, fine_out, field_out):
    lanes = root_out.shape[1]
    first = lax.axis_index("sub") * lanes
    tile = pl.multiple_of(lax.div(first, 128) * 128, 128)
    shift = lax.rem(128 - (first - tile), 128)
    for whole, out in ((root, root_out), (group, group_out)):
        out[...] = pltpu.roll(jnp.broadcast_to(whole[:, pl.ds(tile, 128)], (8, 128)), shift, 1)[0:1, 0:lanes]
    fine_out[...] = fine[...]
    field_out[...] = field[...]


def shape(*dims):
    return jax.ShapeDtypeStruct(dims, F32)


def shards(basis, observations, counts, noise_prec, prior_fine, prior_group, prior_root):
    slots = basis.shape[1]
    nsub, ngrp = lax.axis_size("sub"), lax.axis_size("grp")

    def buf(*dims, kind=F32):
        return pltpu.VMEM(dims, kind)

    def halves(one, two, lanes):
        sizes = (one, two)
        return (
            [buf(SIDE, SIDE, size, lanes) for size in sizes] + [buf(SIDE, size, lanes) for size in sizes]
            + [buf(SIDE, size, lanes) for size in sizes]
        )

    root, group, fine, field = pl.pallas_call(
        kernel,
        name="levels",
        out_shape=[shape(1, R), shape(1, R), shape(1, R), shape(1, slots)],
        in_specs=[SM, SM, VM, HB, HB, HB, HB],
        out_specs=[VM] * 4,
        scratch_shapes=[
            buf(3, slots, R, kind=BF), buf(R, R), buf(128, 128), buf(R, R), buf(R, R), buf(AUG, R),
            buf(2 * R, R, kind=BF), buf(2 * R, R, kind=BF), buf(16, R),
            buf(R, R), buf(SIDE, SIDE, R // nsub, R), buf(R, R), buf(16, R), buf(16, R),
            buf(R, R), buf(SIDE, SIDE, R // nsub, R), buf(8, R), buf(8, R),
            buf(PIECE, 128), buf(ngrp, PIECE, 128), buf(SIDE, SIDE, PIECE, 128),
            [buf(SIDE, SIDE, PIECE, 128), *halves(CUT, PIECE - CUT, 128), buf(SIDE, SIDE, PIECE, 128)],
            halves(R // nsub // 2, R // nsub // 2, R),
            [buf(SIDE, SIDE, PIECE, 128), *halves(CUT, PIECE - CUT, 128)],
            pltpu.SemaphoreType.DMA((7,)),
            pltpu.SemaphoreType.DMA((3, 5, 2, SIDE)), pltpu.SemaphoreType.DMA((3, 5, 2, SIDE)),
            pltpu.SemaphoreType.DMA((2, nsub)), pltpu.SemaphoreType.DMA((2, nsub)),
            pltpu.SemaphoreType.DMA((ngrp,)), pltpu.SemaphoreType.DMA((ngrp,)),
        ],
        compiler_params=pltpu.CompilerParams(collective_id=0, has_side_effects=True, vmem_limit_bytes=60 << 20),
    )(counts, noise_prec, observations.reshape(slots // 128, 128), basis, prior_fine, prior_group, prior_root)
    outs = pl.pallas_call(
        place_kernel,
        name="place",
        out_shape=[shape(1, R // nsub), shape(1, R // nsub), shape(1, R), shape(1, slots)],
        in_specs=[VM] * 4,
        out_specs=[VM] * 4,
    )(root, group, fine, field)
    return tuple(out[0] for out in outs)


def solution(mesh):
    in_specs = (
        P(None, ("grp", "sub"), None),
        P(("grp", "sub")),
        P(("grp", "sub")),
        P(("grp", "sub")),
        P(("grp", "sub"), None, None),
        P("grp", None, None),
        P(),
    )
    out_specs = (P("sub"), P(("grp", "sub")), P(("grp", "sub")), P(("grp", "sub")))
    return jax.shard_map(shards, mesh=mesh, in_specs=in_specs, out_specs=out_specs, check_vma=False)
```
